512 devices in a mesh: row: 16 (over z_lo, core), col: 32 (over x, y, z_hi).
Axes of the slice: x: 4, y: 4, z: 16 (z_hi: 2, z_lo: 8; z = z_hi * 8 + z_lo), core: 2. Of those that a mesh axis runs over, the one named last changes fastest.
Arguments:
- features: bfloat16 [128, 512, 128], P('row', 'col'), may hold values from -6 to 6
- cotangent: bfloat16 [128, 512, 128], P('row', 'col'), may hold values from -12 to 12
- w_qkv: bfloat16 [128, 384], replicated, may hold values from -0.5 to 0.5
- w_out: bfloat16 [128, 128], replicated, may hold values from -0.5 to 0.5
- cos_scale: float32 [2], replicated, may hold values from 4 to 16
Outputs:
- grad_features: bfloat16 [128, 512, 128], P('row', 'col')
- grad_w_qkv: float32 [128, 384], replicated
- grad_w_out: float32 [128, 128], replicated
- grad_scale: float32 [2], replicated
The draws below stay inside these ranges and needn't reach their ends.
All inputs are finite; a program needn't handle non-finite values.
Results may differ from the reference program's by a relative error of at most 0.0085.
Values may be sent and summed in bfloat16 or wider, within the bound.
No kernel may reach another device: no remote copies, remote signals or barrier semaphores. Data moves between devices by JAX's collectives and lax.ppermute only.
A program may use at most 128 MiB of HBM per device.

```python
import math
from functools import reduce
import jax
import jax.numpy as jnp
from jax import lax

D = 128
HEADS = 2
HEAD_DIM = 64
RADIUS = 3
TH = 8
H = 128
W = 512


def draw_cotangent(key, part):
    key = jax.random.fold_in(key, 7)
    row_level = jnp.arange(H, dtype=jnp.float32)[:, None, None] / H
    col_level = jnp.arange(W, dtype=jnp.float32)[None, :, None] / W
    level = jnp.exp(jnp.log(3.0) * (row_level + col_level - 1.0))
    base = jax.random.normal(key, (H, W, D), jnp.float32)
    return jnp.clip(level * base, -12.0, 12.0).astype(jnp.bfloat16)


def level_of(stream_key, extent, shards, smallest, high):
    def one(dim, shards_of):
        steps = jax.random.uniform(jax.random.fold_in(jax.random.fold_in(stream_key, 6), dim), (shards_of,), jnp.float32, smallest / len(shards), high / len(shards))
        return jnp.repeat(jnp.exp(steps), extent[dim] // shards_of).reshape((-1,) + (1,) * (len(extent) - dim - 1))

    level = one(*shards[0])
    for cut in shards[1:]:
        level = level * one(*cut)
    return level


def scatter_about(key, shape, scale, bound, pieces=(), kind=jnp.bfloat16):
    values = scale * jax.random.normal(key, shape, jnp.float32)
    if pieces:
        values = values * level_of(key, shape, pieces, -0.22, 0.18)
    return jnp.clip(values, -bound, bound).astype(kind)


def setup_inputs(seed: int = 0) -> dict:
    key_of = jax.random.split(jax.random.key(seed), 6)
    return {
        "features": scatter_about(key_of[0], (H, W, D), 1.0, 6.0, ((0, 16), (1, 32))),
        "cotangent": draw_cotangent(jax.random.fold_in(key_of[5], 71), 0),
        "w_qkv": scatter_about(key_of[2], (D, 3 * D), D ** -0.5, 0.5),
        "w_out": scatter_about(key_of[3], (D, D), D ** -0.5, 0.5),
        "cos_scale": jnp.clip(jnp.exp(jax.random.uniform(key_of[4], (HEADS,), jnp.float32, math.log(4.0), math.log(16.0))), 4.0, 16.0),
    }


EPSILON = 1e-06

def head_view(values):
    return values.reshape(values.shape[:-1] + (HEADS, HEAD_DIM))

def flat_view(values):
    return values.reshape(values.shape[:-2] + (HEADS * HEAD_DIM,))

def unit_heads(values):
    head_parts = head_view(values.astype(jnp.float32))
    inverse = lax.rsqrt(lax.optimization_barrier(jnp.sum(head_parts * head_parts, axis=-1, keepdims=True)) + EPSILON)
    return (head_parts * inverse, inverse)

def unit_backward(grad_unit, unit, inverse):
    along_unit = lax.optimization_barrier(jnp.sum(unit * grad_unit, axis=-1, keepdims=True))
    return (grad_unit - unit * along_unit) * inverse

def window_pass(q_unit, k_unit, values, d_attn, inside, cos_scale):
    out_rows = q_unit.shape[0]
    out_cols = q_unit.shape[1]
    window_span = 2 * RADIUS + 1
    factor = cos_scale[None, None, :]
    spread = cos_scale[None, None, :, None]
    places = [(shift_row, shift_col) for shift_row in range(window_span) for shift_col in range(window_span)]
    cosines = []
    expos = []
    for shift_row, shift_col in places:
        key_slice = k_unit[shift_row:shift_row + out_rows, shift_col:shift_col + out_cols]
        cosine = lax.optimization_barrier(jnp.sum(q_unit * key_slice, axis=-1))
        live_mask = inside[shift_row:shift_row + out_rows, shift_col:shift_col + out_cols][:, :, None]
        cosines.append(cosine)
        expos.append(jnp.where(live_mask, jnp.exp(factor * cosine), 0.0))
    denominator = reduce(jnp.add, expos)
    weights = [expo / denominator for expo in expos]
    mixed_out = jnp.zeros(q_unit.shape, jnp.float32)
    dot_terms = []
    for position, (shift_row, shift_col) in enumerate(places):
        value_slice = values[shift_row:shift_row + out_rows, shift_col:shift_col + out_cols]
        mixed_out = mixed_out + weights[position][..., None] * value_slice
        dot_terms.append(lax.optimization_barrier(jnp.sum(d_attn * value_slice, axis=-1)))
    center = reduce(jnp.add, [weights[position] * dot_terms[position] for position in range(len(places))])
    grad_q = jnp.zeros(q_unit.shape, jnp.float32)
    grad_k = jnp.zeros(k_unit.shape, jnp.float32)
    grad_v = jnp.zeros(values.shape, jnp.float32)
    scale_terms = jnp.zeros(cosines[0].shape, jnp.float32)
    for position, (shift_row, shift_col) in enumerate(places):
        key_slice = k_unit[shift_row:shift_row + out_rows, shift_col:shift_col + out_cols]
        grad_score = weights[position] * (dot_terms[position] - center)
        scale_terms = scale_terms + grad_score * cosines[position]
        grad_q = grad_q + spread * grad_score[..., None] * key_slice
        grad_k = grad_k.at[shift_row:shift_row + out_rows, shift_col:shift_col + out_cols].add(spread * grad_score[..., None] * q_unit)
        grad_v = grad_v.at[shift_row:shift_row + out_rows, shift_col:shift_col + out_cols].add(weights[position][..., None] * d_attn)
    return (mixed_out, grad_q, grad_k, grad_v, scale_terms)

def reference(features, cotangent, w_qkv, w_out, cos_scale):
    rows_all, cols_all, model_width = features.shape
    margin = RADIUS
    padded_in = jnp.pad(features, ((2 * margin, 2 * margin), (margin, margin), (0, 0)))
    padded_grad = jnp.pad(cotangent, ((margin, margin), (0, 0), (0, 0)))
    col_here = jnp.arange(cols_all + 2 * margin, dtype=jnp.int32) - margin
    col_valid = (col_here >= 0) & (col_here < cols_all)

    def band(band_index):
        band_start = band_index * TH
        block_in = lax.dynamic_slice_in_dim(padded_in, band_start, TH + 4 * margin, 0)
        block_grad = lax.dynamic_slice_in_dim(padded_grad, band_start, TH + 2 * margin, 0)
        rows_here = band_start - 2 * margin + jnp.arange(TH + 4 * margin, dtype=jnp.int32)
        row_valid = (rows_here >= 0) & (rows_here < rows_all)
        inside = row_valid[:, None] & col_valid[None, :]
        projected = jnp.dot(block_in.reshape(-1, model_width), w_qkv, preferred_element_type=jnp.float32)
        projected = projected.astype(jnp.bfloat16).reshape(TH + 4 * margin, cols_all + 2 * margin, 3 * model_width)
        query_raw = projected[margin:margin + TH + 2 * margin, margin:margin + cols_all, :model_width]
        q_unit, q_inverse = unit_heads(query_raw)
        k_unit, k_inverse = unit_heads(projected[:, :, model_width:2 * model_width])
        values = head_view(projected[:, :, 2 * model_width:].astype(jnp.float32))
        d_attn = jnp.dot(block_grad.reshape(-1, model_width), w_out.T, preferred_element_type=jnp.float32)
        d_attn = d_attn.astype(jnp.bfloat16).reshape(TH + 2 * margin, cols_all, model_width)
        mixed_out, grad_q, grad_k, grad_v, scale_terms = window_pass(q_unit, k_unit, values, head_view(d_attn.astype(jnp.float32)), inside, cos_scale)
        attn_out = flat_view(mixed_out[margin:margin + TH]).astype(jnp.bfloat16).reshape(-1, model_width)
        grad_own = block_grad[margin:margin + TH].reshape(-1, model_width)
        out_part = jnp.dot(attn_out.T, grad_own, preferred_element_type=jnp.float32)
        scale_part = lax.optimization_barrier(jnp.sum(scale_terms[margin:margin + TH], axis=(0, 1)))
        key_rows = slice(2 * margin, 2 * margin + TH)
        key_cols = slice(margin, margin + cols_all)
        grad_key = unit_backward(grad_k[key_rows, key_cols], k_unit[key_rows, key_cols], k_inverse[key_rows, key_cols])
        grad_query = unit_backward(grad_q[margin:margin + TH], q_unit[margin:margin + TH], q_inverse[margin:margin + TH])
        grad_proj = jnp.concatenate([flat_view(grad_query), flat_view(grad_key), flat_view(grad_v[key_rows, key_cols])], axis=-1)
        grad_proj = grad_proj.astype(jnp.bfloat16).reshape(-1, 3 * model_width)
        own_in = block_in[key_rows, key_cols].reshape(-1, model_width)
        grad_in = jnp.dot(grad_proj, w_qkv.T, preferred_element_type=jnp.float32).astype(jnp.bfloat16)
        qkv_part = jnp.dot(own_in.T, grad_proj, preferred_element_type=jnp.float32)
        return (grad_in.reshape(TH, cols_all, model_width), qkv_part, out_part, scale_part)
    grad_bands, qkv_parts, out_parts, scale_parts = lax.map(band, jnp.arange(rows_all // TH, dtype=jnp.int32))
    grad_norm = float(rows_all * cols_all) ** (-0.5)
    grad_features = grad_bands.reshape(rows_all, cols_all, model_width)
    return (grad_features, lax.optimization_barrier(jnp.sum(qkv_parts, axis=0)) * grad_norm, lax.optimization_barrier(jnp.sum(out_parts, axis=0)) * grad_norm, lax.optimization_barrier(jnp.sum(scale_parts, axis=0)) * grad_norm)
```

```python
import functools

import jax
import jax.numpy as jnp
import numpy as np
from jax import lax
from jax.experimental import pallas as pl
from jax.experimental.pallas import tpu as pltpu
from jax.sharding import Mesh
from jax.sharding import PartitionSpec as P

RADIUS = 3
EPSILON = 1e-06
MODEL = 128
HEAD = 64
ROWS, COLS = 8, 16
OWN = ROWS * COLS
QUERIES = 352
KEYS = 640
NEAR = 384
BLOCK = 32
SHARES = 32
LOG2E = 1.4426950408889634
FAR_AWAY = 1e4

F32 = jnp.float32
BF16 = jnp.bfloat16


def side_columns(left, inner):
    if left:
        return -3 if inner else -6
    return 16 if inner else 19


def token_table(core):
    def tile(holder, start, count, lift):
        token = start + np.arange(count)
        return np.stack([8 * holder + token // 16 + lift, token % 16])

    def edge(start, count, left, inner, lift):
        token = start + np.arange(count)
        return np.stack([token // 3 + lift, token % 3 + side_columns(left, inner)])

    other = 1 - core
    lift = -16 if core == 0 else 16
    far_left = core == 0
    sent_left = other == 0
    pieces = [
        tile(core, 0, 128, 0),
        tile(other, 80 * core, 48, 0),
        edge(0, 48, far_left, True, 0),
        edge(0, 48, not far_left, True, 0),
        tile(other, 80 * other, 48, lift),
        edge(32 * other, 16, sent_left, True, lift),
        edge(32 * other, 16, not sent_left, True, lift),
        tile(other, 48 - 16 * core, 48, 0),
        edge(0, 48, far_left, False, 0),
        edge(0, 48, not far_left, False, 0),
        tile(other, 48 - 16 * other, 48, lift),
        edge(16, 16, sent_left, True, lift),
        edge(16 * other, 32, sent_left, False, lift),
        edge(16, 16, not sent_left, True, lift),
        edge(16 * other, 32, not sent_left, False, lift),
    ]
    return np.concatenate(pieces, axis=1).astype(np.float32)


TABLES = np.stack([token_table(0), token_table(1)])


def vmem(count):
    return [pl.BlockSpec(memory_space=pltpu.VMEM)] * count


def dot_nt(left, right):
    return lax.dot_general(
        left, right, (((1,), (1,)), ((), ())), preferred_element_type=F32
    )


def dot_tn(left, right):
    return lax.dot_general(
        left, right, (((0,), (0,)), ((), ())), preferred_element_type=F32
    )


def dot_nn(left, right):
    return jnp.dot(left, right, preferred_element_type=F32)


def far_kernel(place, feat, cot, other_feat, other_cot, out):
    core = place[0]
    spot = lax.broadcasted_iota(jnp.int32, (96, 128), 0)
    token = lax.broadcasted_iota(jnp.int32, (96, 128), 1)
    outer = jnp.where(spot >= 48, 1, 0)
    index = spot - 48 * outer
    row = (index * 43) >> 7
    step = index - 3 * row
    column = step + jnp.where(core == 0, 13 - 3 * outer, 3 * outer)
    half = row >> 3
    wanted = (row - 8 * half) * 16 + column
    mine = jnp.where((wanted == token) & (half == core), 1.0, 0.0).astype(BF16)
    theirs = jnp.where((wanted == token) & (half != core), 1.0, 0.0).astype(BF16)
    out[0:96, :] = (dot_nn(mine, feat[...]) + dot_nn(theirs, other_feat[...])).astype(BF16)
    out[96:144, :] = (
        dot_nn(mine[0:48], cot[...]) + dot_nn(theirs[0:48], other_cot[...])
    ).astype(BF16)


def rows_at(ref, start, count):
    return ref[pl.ds(pl.multiple_of(start, 16), count), :]


def vertical_kernel(place, feat, cot, far, swapped, out):
    core = place[0]
    out[0:48, :] = rows_at(feat, 80 * core, 48)
    out[48:64, :] = rows_at(far, 32 * core, 16)
    out[64:80, :] = rows_at(swapped, 32 * core, 16)
    out[80:128, :] = rows_at(feat, 48 - 16 * core, 48)
    out[128:144, :] = far[16:32, :]
    out[144:176, :] = rows_at(far, 48 + 16 * core, 32)
    out[176:192, :] = swapped[16:32, :]
    out[192:224, :] = rows_at(swapped, 48 + 16 * core, 32)
    out[224:272, :] = rows_at(cot, 80 * core, 48)
    out[272:288, :] = rows_at(far, 96 + 32 * core, 16)
    out[288:304, :] = rows_at(swapped, 96 + 32 * core, 16)


def attention_kernel(
    place,
    cos_scale,
    feat,
    cot,
    other_feat,
    other_cot,
    far,
    swapped,
    vertical,
    w_qkv,
    w_out,
    key_spots,
    query_spots,
    grad_feat,
    grad_w,
    grad_scale,
    tokens,
    cots,
    keys,
    values,
    queries,
    d_attn,
    raw,
    dots,
    bias,
    mix_own,
    mix_key,
    slope_own,
    slope_key,
):
    core = place[0]
    tokens[0:128, :] = feat[...]
    tokens[128:176, :] = rows_at(other_feat, 80 * core, 48)
    tokens[176:224, :] = far[0:48, :]
    tokens[224:272, :] = swapped[0:48, :]
    tokens[272:352, :] = vertical[0:80, :]
    tokens[352:400, :] = rows_at(other_feat, 48 - 16 * core, 48)
    tokens[400:448, :] = far[48:96, :]
    tokens[448:496, :] = swapped[48:96, :]
    tokens[496:640, :] = vertical[80:224, :]
    cots[0:128, :] = cot[...]
    cots[128:176, :] = rows_at(other_cot, 80 * core, 48)
    cots[176:224, :] = far[96:144, :]
    cots[224:272, :] = swapped[96:144, :]
    cots[272:352, :] = vertical[224:304, :]

    keys[...] = dot_nn(tokens[...], w_qkv[:, MODEL : 2 * MODEL]).astype(BF16)
    values[...] = dot_nn(tokens[...], w_qkv[:, 2 * MODEL :]).astype(BF16)
    queries[...] = dot_nn(tokens[0:QUERIES, :], w_qkv[:, :MODEL]).astype(BF16)
    d_attn[...] = dot_nt(cots[...], w_out[...]).astype(BF16)

    spots = key_spots[pl.ds(core, 1)].reshape(8, KEYS)
    key_rows, key_cols = spots[0:1, :], spots[1:2, :]
    all_rows = key_rows + place[1].astype(F32)
    all_cols = key_cols + place[2].astype(F32)
    inside = (all_rows >= 0) & (all_rows < 128) & (all_cols >= 0) & (all_cols < 512)
    key_rows = jnp.where(inside, key_rows, FAR_AWAY)
    for start in range(0, QUERIES, BLOCK):
        here = query_spots[pl.ds(core, 1), start : start + BLOCK, :].reshape(BLOCK, 8)
        apart = jnp.maximum(
            jnp.abs(here[:, 0:1] - key_rows), jnp.abs(here[:, 1:2] - key_cols)
        )
        bias[start : start + BLOCK, :] = jnp.where(apart <= RADIUS, 0.0, -1e30)

    key_wide = keys[...].astype(F32)
    square = key_wide * key_wide
    upper = square.astype(BF16)
    lower = (square - upper.astype(F32)).astype(BF16)
    head_of = lax.broadcasted_iota(jnp.int32, (16, MODEL), 1) // HEAD
    picks = jnp.where(
        head_of == lax.broadcasted_iota(jnp.int32, (16, MODEL), 0), 1.0, 0.0
    ).astype(BF16)
    key_inverse = lax.rsqrt(dot_nt(picks, upper) + dot_nt(picks, lower) + EPSILON)

    first = lax.broadcasted_iota(jnp.int32, (1, MODEL), 1) < HEAD

    def head_sums(array):
        low = jnp.sum(jnp.where(first, array, 0.0), axis=1, keepdims=True)
        high = jnp.sum(jnp.where(first, 0.0, array), axis=1, keepdims=True)
        return low, high

    for head in range(2):
        own_lanes = first if head == 0 else ~first
        raw[head] = dot_nt(jnp.where(own_lanes, queries[...], 0.0).astype(BF16), keys[...])
        dots[head] = dot_nt(jnp.where(own_lanes, d_attn[...], 0.0).astype(BF16), values[...])

    scale_sums = [jnp.zeros((BLOCK, 1), F32), jnp.zeros((BLOCK, 1), F32)]
    for start in range(0, QUERIES, BLOCK):
        rows = slice(start, start + BLOCK)
        query_wide = queries[rows, :].astype(F32)
        norms = head_sums(query_wide * query_wide)
        for head in range(2):
            inverse = lax.rsqrt(norms[head] + EPSILON)
            reach = inverse * cos_scale[head]
            key_inv = key_inverse[head : head + 1, :]
            score = raw[head, rows, :] * (reach * LOG2E) * key_inv + bias[rows, :]
            expo = jnp.exp2(score)
            gain = dots[head, rows, :]
            share = 1.0 / (jnp.sum(expo, axis=1, keepdims=True) + 1e-30)
            center = jnp.sum(expo * gain, axis=1, keepdims=True) * share
            if start < OWN:
                weight = expo[:, :NEAR] * share
                slope = weight * (gain[:, :NEAR] - center)
                pull = slope * key_inv[:, :NEAR]
                scale_sums[head] += inverse * jnp.sum(
                    pull * raw[head, rows, :NEAR], axis=1, keepdims=True
                )
                mix_own[head, rows, :] = weight.astype(BF16)
                slope_own[head, rows, :] = (pull * cos_scale[head]).astype(BF16)
                weight = weight[:, :OWN]
                slope = slope[:, :OWN]
            else:
                weight = expo[:, :OWN] * share
                slope = weight * (gain[:, :OWN] - center)
            mix_key[head, rows, :] = weight.astype(BF16)
            slope_key[head, rows, :] = (slope * reach).astype(BF16)

    def both(dot, left, right):
        return jnp.where(first, dot(left[0], right), dot(left[1], right))

    attn_out = both(dot_nn, mix_own, values[0:NEAR, :]).astype(BF16)
    dq_unit = both(dot_nn, slope_own, keys[0:NEAR, :])
    dk_unit = both(dot_tn, slope_key, queries[...])
    dv = both(dot_tn, mix_key, d_attn[...])

    def unit_backward(vector, grad_unit):
        low, high = head_sums(vector * vector)
        inverse = jnp.where(first, lax.rsqrt(low + EPSILON), lax.rsqrt(high + EPSILON))
        unit = vector * inverse
        low, high = head_sums(unit * grad_unit)
        return (grad_unit - unit * jnp.where(first, low, high)) * inverse

    dq = unit_backward(queries[0:OWN, :].astype(F32), dq_unit).astype(BF16)
    dk = unit_backward(keys[0:OWN, :].astype(F32), dk_unit).astype(BF16)
    dv = dv.astype(BF16)
    grad_feat[...] = (
        dot_nt(dq, w_qkv[:, :MODEL])
        + dot_nt(dk, w_qkv[:, MODEL : 2 * MODEL])
        + dot_nt(dv, w_qkv[:, 2 * MODEL :])
    ).astype(BF16)
    norm = 1.0 / 256.0
    for part, grad in enumerate((dq, dk, dv)):
        grad_w[part * MODEL : (part + 1) * MODEL, :] = (
            dot_tn(feat[...], grad) * norm
        ).astype(BF16)
    grad_w[3 * MODEL :, :] = (dot_tn(attn_out, cot[...]) * norm).astype(BF16)

    lane = lax.broadcasted_iota(jnp.int32, (8, MODEL), 1)
    held = jnp.zeros((8, MODEL), F32)
    for head in range(2):
        rest = jnp.sum(scale_sums[head], axis=0, keepdims=True) * norm
        for part in range(3):
            piece = rest.astype(BF16).astype(F32)
            held = jnp.where(lane == 3 * head + part, piece, held)
            rest = rest - piece
    grad_scale[...] = held.astype(BF16)


def pairs(target):
    found = []
    for row in range(16):
        for col in range(32):
            to_row, to_col = target(row, col)
            if 0 <= to_row < 16 and 0 <= to_col < 32:
                found.append((row * 32 + col, to_row * 32 + to_col))
    return found


EVERY = ("lo", "core", "x", "y", "hi")
PLANE = ("x", "y", "core")
LINE = ("lo", "hi")
CHIP_MATE = pairs(lambda row, col: (row ^ 1, col))
FAR_MATE = pairs(lambda row, col: (row, col - 1 if row % 2 else col + 1))
NEXT_CHIP = pairs(lambda row, col: (row + 1 if row % 2 else row - 1, col))


def exchange(array, axes):
    return lax.all_to_all(array, axes, 0, 0, tiled=True)


def to_all(array, axes, count):
    return exchange(jnp.broadcast_to(array[None], (count,) + array.shape), axes)


def on_device(features, cotangent, w_qkv, w_out, cos_scale):
    core = lax.axis_index("core")
    col = lax.axis_index(("x", "y", "hi"))
    place = jnp.stack([core, lax.axis_index("lo") * 16, col * 16]).astype(jnp.int32)
    feat = features.reshape(OWN, MODEL)
    cot = cotangent.reshape(OWN, MODEL)
    smem = pl.BlockSpec(memory_space=pltpu.SMEM)

    other = lax.ppermute(jnp.stack([feat, cot]), EVERY, CHIP_MATE)
    other_feat, other_cot = other[0], other[1]
    far_out = pl.pallas_call(
        far_kernel,
        out_shape=jax.ShapeDtypeStruct((144, MODEL), BF16),
        in_specs=[smem] + vmem(4),
        out_specs=vmem(1)[0],
        name="far_edges",
    )(place, feat, cot, other_feat, other_cot)
    far = lax.ppermute(far_out, EVERY, FAR_MATE)
    swapped = lax.ppermute(far, EVERY, CHIP_MATE)
    vertical_out = pl.pallas_call(
        vertical_kernel,
        out_shape=jax.ShapeDtypeStruct((304, MODEL), BF16),
        in_specs=[smem] + vmem(4),
        out_specs=vmem(1)[0],
        name="vertical_edges",
    )(place, feat, cot, far, swapped)
    vertical = lax.ppermute(vertical_out, EVERY, NEXT_CHIP)

    key_spots = np.zeros((2, 8, KEYS), np.float32)
    key_spots[:, :2] = TABLES
    query_spots = np.zeros((2, QUERIES, 8), np.float32)
    query_spots[:, :, :2] = TABLES[:, :, :QUERIES].transpose(0, 2, 1)
    grad_feat, grad_w, scale_tile = pl.pallas_call(
        attention_kernel,
        out_shape=(
            jax.ShapeDtypeStruct((OWN, MODEL), BF16),
            jax.ShapeDtypeStruct((4 * MODEL, MODEL), BF16),
            jax.ShapeDtypeStruct((8, MODEL), BF16),
        ),
        in_specs=[smem, smem] + vmem(11),
        out_specs=vmem(3),
        scratch_shapes=[
            pltpu.VMEM((KEYS, MODEL), BF16),
            pltpu.VMEM((QUERIES, MODEL), BF16),
            pltpu.VMEM((KEYS, MODEL), BF16),
            pltpu.VMEM((KEYS, MODEL), BF16),
            pltpu.VMEM((QUERIES, MODEL), BF16),
            pltpu.VMEM((QUERIES, MODEL), BF16),
            pltpu.VMEM((2, QUERIES, KEYS), F32),
            pltpu.VMEM((2, QUERIES, KEYS), F32),
            pltpu.VMEM((QUERIES, KEYS), F32),
            pltpu.VMEM((2, OWN, NEAR), BF16),
            pltpu.VMEM((2, QUERIES, OWN), BF16),
            pltpu.VMEM((2, OWN, NEAR), BF16),
            pltpu.VMEM((2, QUERIES, OWN), BF16),
        ],
        compiler_params=pltpu.CompilerParams(vmem_limit_bytes=32 * 1024 * 1024),
        name="window_attention",
    )(
        place,
        cos_scale,
        feat,
        cot,
        other_feat,
        other_cot,
        far,
        swapped,
        vertical,
        w_qkv,
        w_out,
        jnp.asarray(key_spots),
        jnp.asarray(query_spots),
    )

    scale_rows = jnp.broadcast_to(scale_tile[None], (SHARES, 8, MODEL))
    shares = jnp.concatenate([grad_w.reshape(SHARES, 16, MODEL), scale_rows], axis=1)
    share = jnp.sum(exchange(shares, PLANE).astype(F32), axis=0)
    pieces = share[16:17, 0:6].reshape(2, 3)
    scale_part = jnp.sum(pieces, axis=1, keepdims=True)
    top = lax.reduce_precision(scale_part, 8, 7)
    middle = lax.reduce_precision(scale_part - top, 8, 7)
    split = jnp.concatenate([top, middle, scale_part - top - middle], axis=1)
    split = jnp.pad(split.reshape(1, 6), ((0, 7), (0, MODEL - 6)))
    share = jnp.concatenate([share[:16], split], axis=0).astype(BF16)
    share = jnp.sum(to_all(share, LINE, 16).astype(F32), axis=0)
    grad_scale = jnp.sum(share[16, 0:6].reshape(2, 3), axis=1)
    whole = to_all(share[:16].astype(BF16), PLANE, SHARES).astype(F32)
    whole = whole.reshape(4, MODEL, MODEL)
    grad_w_qkv = jnp.concatenate([whole[0], whole[1], whole[2]], axis=1)
    return (grad_feat.reshape(ROWS, COLS, MODEL), grad_w_qkv, whole[3], grad_scale)


def solution(mesh):
    fine = Mesh(mesh.devices.reshape(8, 2, 4, 4, 2), EVERY)
    tokens = P(("lo", "core"), ("x", "y", "hi"), None)
    return jax.shard_map(
        on_device,
        mesh=fine,
        in_specs=(tokens, tokens, P(), P(), P()),
        out_specs=(tokens, P(), P(), P()),
        check_vma=False,
    )
```

```python
import functools

import jax
import jax.numpy as jnp
import numpy as np
from jax import lax
from jax.experimental import pallas as pl
from jax.experimental.pallas import tpu as pltpu
from jax.sharding import PartitionSpec as P

RADIUS = 3
EPSILON = 1e-06
MODEL = 128
HEAD = 64
ROWS, COLS = 8, 16
OWN = ROWS * COLS
QUERIES = 368
KEYS = 640
NEAR = 384
BLOCK = 16
EDGE = 24
SENT = 80
SHARES = 32
LOG2E = 1.4426950408889634
FAR_AWAY = 1e4

F32 = jnp.float32
BF16 = jnp.bfloat16


def side_columns(left, inner):
    if left:
        return -3 if inner else -6
    return 16 if inner else 19


def token_table(core):
    def tile(holder, start, count, lift):
        token = start + np.arange(count)
        return np.stack([8 * holder + token // 16 + lift, token % 16])

    def edge(holder, left, inner, lift):
        token = np.arange(EDGE)
        row = 8 * holder + token // 3 + lift
        return np.stack([row, token % 3 + side_columns(left, inner)])

    other = 1 - core
    lift = -16 if core == 0 else 16
    left = core == 0
    pieces = [
        tile(core, 0, 128, 0),
        tile(other, 80 * core, 48, 0),
        edge(core, left, True, 0),
        edge(other, left, True, 0),
        edge(other, not left, True, 0),
        edge(core, not left, True, 0),
        tile(other, 80 * other, 48, lift),
        edge(other, not left, True, lift),
        edge(other, left, True, lift),
        tile(other, 48 - 16 * core, 48, 0),
        edge(core, left, False, 0),
        edge(other, left, False, 0),
        edge(other, not left, False, 0),
        edge(core, not left, False, 0),
        tile(other, 48 - 16 * other, 48, lift),
        edge(other, not left, False, lift),
        edge(other, left, False, lift),
        np.full((2, 32), FAR_AWAY),
    ]
    return np.concatenate(pieces, axis=1).astype(np.float32)


TABLES = np.stack([token_table(0), token_table(1)])


def vmem(count):
    return [pl.BlockSpec(memory_space=pltpu.VMEM)] * count


def dot_nt(left, right):
    return lax.dot_general(
        left, right, (((1,), (1,)), ((), ())), preferred_element_type=F32
    )


def dot_tn(left, right):
    return lax.dot_general(
        left, right, (((0,), (0,)), ((), ())), preferred_element_type=F32
    )


def dot_nn(left, right):
    return jnp.dot(left, right, preferred_element_type=F32)


def edge_kernel(place, feat, cot, own_edge, mate_edge, tile):
    core = place[0]
    spot = lax.broadcasted_iota(jnp.int32, (SENT, 128), 0)
    token = lax.broadcasted_iota(jnp.int32, (SENT, 128), 1)
    kind = jnp.where(spot >= EDGE, 1, 0) + jnp.where(spot >= 2 * EDGE, 1, 0)
    index = spot - EDGE * kind
    row = (index * 43) >> 7
    step = index - 3 * row
    outer = kind == 1
    right = row * 16 + step + jnp.where(outer, 10, 13)
    left = row * 16 + step + jnp.where(outer, 3, 0)
    used = spot < 3 * EDGE
    from_cot = kind == 2
    for ref, wanted in (
        (own_edge, jnp.where(core == 0, right, left)),
        (mate_edge, jnp.where(core == 0, left, right)),
    ):
        hit = (wanted == token) & used
        of_feat = jnp.where(hit & ~from_cot, 1.0, 0.0).astype(BF16)
        of_cot = jnp.where(hit & from_cot, 1.0, 0.0).astype(BF16)
        ref[...] = (dot_nn(of_feat, feat[...]) + dot_nn(of_cot, cot[...])).astype(BF16)
    tile[0:OWN, :] = feat[...]
    tile[OWN:, :] = cot[...]


def rows_at(ref, start, count):
    return ref[pl.ds(pl.multiple_of(start, 16), count), :]


def attention_kernel(
    place,
    cos_scale,
    feat,
    cot,
    mate,
    next_chip,
    far,
    far_mate,
    far_next,
    far_skip,
    w_qkv,
    w_out,
    key_spots,
    query_spots,
    grad_feat,
    grad_w,
    grad_scale,
    tokens,
    cots,
    keys,
    values,
    queries,
    d_attn,
    raw,
    dots,
    bias,
    mix_own,
    mix_key,
    slope_own,
    slope_key,
):
    core = place[0]
    other = 1 - core
    far_wide = far[...].astype(F32)
    mate_wide = far_mate[...].astype(F32)
    next_wide = far_next[0:SENT, :].astype(F32)
    skip_wide = far_skip[SENT:, :].astype(F32)
    edges = (
        far_wide[:SENT],
        far_wide[SENT:],
        mate_wide[:SENT],
        mate_wide[SENT:],
        next_wide,
        skip_wide,
    )

    def strip(kind, chosen):
        pieces = [edge[kind * EDGE : (kind + 1) * EDGE] for edge in chosen]
        return jnp.concatenate(pieces, axis=0).astype(BF16)

    tokens[0:128, :] = feat[...]
    tokens[128:176, :] = rows_at(mate, 80 * core, 48)
    tokens[176:272, :] = strip(0, edges[:4])
    tokens[272:320, :] = rows_at(next_chip, 80 * other, 48)
    tokens[320:368, :] = strip(0, edges[4:])
    tokens[368:416, :] = rows_at(mate, 48 - 16 * core, 48)
    tokens[416:512, :] = strip(1, edges[:4])
    tokens[512:560, :] = rows_at(next_chip, 48 - 16 * other, 48)
    tokens[560:608, :] = strip(1, edges[4:])
    tokens[608:640, :] = jnp.zeros((32, MODEL), BF16)
    cots[0:128, :] = cot[...]
    cots[128:176, :] = rows_at(mate, OWN + 80 * core, 48)
    cots[176:272, :] = strip(2, edges[:4])
    cots[272:320, :] = rows_at(next_chip, OWN + 80 * other, 48)
    cots[320:368, :] = strip(2, edges[4:])

    keys[...] = dot_nn(tokens[...], w_qkv[:, MODEL : 2 * MODEL]).astype(BF16)
    values[...] = dot_nn(tokens[...], w_qkv[:, 2 * MODEL :]).astype(BF16)
    queries[...] = dot_nn(tokens[0:QUERIES, :], w_qkv[:, :MODEL]).astype(BF16)
    d_attn[...] = dot_nt(cots[...], w_out[...]).astype(BF16)

    spots = key_spots[pl.ds(core, 1)].reshape(8, KEYS)
    key_rows, key_cols = spots[0:1, :], spots[1:2, :]
    all_rows = key_rows + place[1].astype(F32)
    all_cols = key_cols + place[2].astype(F32)
    inside = (all_rows >= 0) & (all_rows < 128) & (all_cols >= 0) & (all_cols < 512)
    key_rows = jnp.where(inside, key_rows, FAR_AWAY)
    for start in range(0, QUERIES, BLOCK):
        here = query_spots[pl.ds(core, 1), start : start + BLOCK, :].reshape(BLOCK, 8)
        apart = jnp.maximum(
            jnp.abs(here[:, 0:1] - key_rows), jnp.abs(here[:, 1:2] - key_cols)
        )
        bias[start : start + BLOCK, :] = jnp.where(apart <= RADIUS, 0.0, -1e30)

    key_wide = keys[...].astype(F32)
    square = key_wide * key_wide
    upper = square.astype(BF16)
    lower = (square - upper.astype(F32)).astype(BF16)
    head_of = lax.broadcasted_iota(jnp.int32, (16, MODEL), 1) // HEAD
    picks = jnp.where(
        head_of == lax.broadcasted_iota(jnp.int32, (16, MODEL), 0), 1.0, 0.0
    ).astype(BF16)
    key_inverse = lax.rsqrt(dot_nt(picks, upper) + dot_nt(picks, lower) + EPSILON)

    first = lax.broadcasted_iota(jnp.int32, (1, MODEL), 1) < HEAD

    def head_sums(array):
        low = jnp.sum(jnp.where(first, array, 0.0), axis=1, keepdims=True)
        high = jnp.sum(jnp.where(first, 0.0, array), axis=1, keepdims=True)
        return low, high

    for head in range(2):
        own_lanes = first if head == 0 else ~first
        raw[head] = dot_nt(jnp.where(own_lanes, queries[...], 0.0).astype(BF16), keys[...])
        dots[head] = dot_nt(jnp.where(own_lanes, d_attn[...], 0.0).astype(BF16), values[...])

    scale_sums = [jnp.zeros((BLOCK, 1), F32), jnp.zeros((BLOCK, 1), F32)]
    for start in range(0, QUERIES, BLOCK):
        rows = slice(start, start + BLOCK)
        query_wide = queries[rows, :].astype(F32)
        norms = head_sums(query_wide * query_wide)
        for head in range(2):
            inverse = lax.rsqrt(norms[head] + EPSILON)
            reach = inverse * cos_scale[head]
            key_inv = key_inverse[head : head + 1, :]
            score = raw[head, rows, :] * (reach * LOG2E) * key_inv + bias[rows, :]
            expo = jnp.exp2(score)
            gain = dots[head, rows, :]
            share = 1.0 / (jnp.sum(expo, axis=1, keepdims=True) + 1e-30)
            center = jnp.sum(expo * gain, axis=1, keepdims=True) * share
            if start < OWN:
                weight = expo[:, :NEAR] * share
                slope = weight * (gain[:, :NEAR] - center)
                pull = slope * key_inv[:, :NEAR]
                scale_sums[head] += inverse * jnp.sum(
                    pull * raw[head, rows, :NEAR], axis=1, keepdims=True
                )
                mix_own[head, rows, :] = weight.astype(BF16)
                slope_own[head, rows, :] = (pull * cos_scale[head]).astype(BF16)
                weight = weight[:, :OWN]
                slope = slope[:, :OWN]
            else:
                weight = expo[:, :OWN] * share
                slope = weight * (gain[:, :OWN] - center)
            mix_key[head, rows, :] = weight.astype(BF16)
            slope_key[head, rows, :] = (slope * reach).astype(BF16)

    def both(dot, left, right):
        return jnp.where(first, dot(left[0], right), dot(left[1], right))

    attn_out = both(dot_nn, mix_own, values[0:NEAR, :]).astype(BF16)
    dq_unit = both(dot_nn, slope_own, keys[0:NEAR, :])
    dk_unit = both(dot_tn, slope_key, queries[...])
    dv = both(dot_tn, mix_key, d_attn[...])

    def unit_backward(vector, grad_unit):
        low, high = head_sums(vector * vector)
        inverse = jnp.where(first, lax.rsqrt(low + EPSILON), lax.rsqrt(high + EPSILON))
        unit = vector * inverse
        low, high = head_sums(unit * grad_unit)
        return (grad_unit - unit * jnp.where(first, low, high)) * inverse

    dq = unit_backward(queries[0:OWN, :].astype(F32), dq_unit).astype(BF16)
    dk = unit_backward(keys[0:OWN, :].astype(F32), dk_unit).astype(BF16)
    dv = dv.astype(BF16)
    grad_feat[...] = (
        dot_nt(dq, w_qkv[:, :MODEL])
        + dot_nt(dk, w_qkv[:, MODEL : 2 * MODEL])
        + dot_nt(dv, w_qkv[:, 2 * MODEL :])
    ).astype(BF16)
    norm = 1.0 / 256.0
    for part, grad in enumerate((dq, dk, dv)):
        grad_w[part * MODEL : (part + 1) * MODEL, :] = (
            dot_tn(feat[...], grad) * norm
        ).astype(BF16)
    grad_w[3 * MODEL :, :] = (dot_tn(attn_out, cot[...]) * norm).astype(BF16)

    lane = lax.broadcasted_iota(jnp.int32, (8, MODEL), 1)
    held = jnp.zeros((8, MODEL), F32)
    for head in range(2):
        rest = jnp.sum(scale_sums[head], axis=0, keepdims=True) * norm
        for part in range(3):
            piece = rest.astype(BF16).astype(F32)
            held = jnp.where(lane == 3 * head + part, piece, held)
            rest = rest - piece
    grad_scale[...] = held.astype(BF16)


def pairs(target):
    found = []
    for row in range(16):
        for col in range(32):
            to_row, to_col = target(row, col)
            if 0 <= to_row < 16 and 0 <= to_col < 32:
                found.append((row * 32 + col, to_row * 32 + to_col))
    return found


EVERY = ("row", "col")


def device(x, y, z, core):
    return ((z % 8) * 2 + core) * 32 + (x % 4) * 8 + (y % 4) * 2 + z // 8 % 2


FIRST_X, FIRST_Y, FIRST_Z = 2, 2, 8
PLANES = [
    [
        device(x + FIRST_X, y + FIRST_Y, z, core)
        for x in range(4)
        for y in range(4)
        for core in range(2)
    ]
    for z in range(16)
]
LINES = [
    [device(x, y, z + FIRST_Z, core) for z in range(16)]
    for x in range(4)
    for y in range(4)
    for core in range(2)
]
CHIP_MATE = pairs(lambda row, col: (row ^ 1, col))
FAR_MATE = pairs(lambda row, col: (row, col - 1 if row % 2 else col + 1))
NEXT_CHIP = pairs(lambda row, col: (row + 1 if row % 2 else row - 1, col))
SKIP_CHIP = pairs(lambda row, col: (row - 2 if row % 2 else row + 2, col))


def exchange(array, groups):
    return lax.all_to_all(array, EVERY, 0, 0, axis_index_groups=groups, tiled=True)


def to_all(array, groups):
    return exchange(jnp.broadcast_to(array[None], (len(groups[0]),) + array.shape), groups)


def on_device(features, cotangent, w_qkv, w_out, cos_scale):
    row, col = lax.axis_index("row"), lax.axis_index("col")
    place = jnp.stack([row % 2, row // 2 * 16, col * 16]).astype(jnp.int32)
    feat = features.reshape(OWN, MODEL)
    cot = cotangent.reshape(OWN, MODEL)
    smem = pl.BlockSpec(memory_space=pltpu.SMEM)

    edge = jax.ShapeDtypeStruct((SENT, MODEL), BF16)
    own_edge, mate_edge, tile = pl.pallas_call(
        edge_kernel,
        out_shape=(edge, edge, jax.ShapeDtypeStruct((2 * OWN, MODEL), BF16)),
        in_specs=[smem] + vmem(2),
        out_specs=vmem(3),
        name="edges",
    )(place, feat, cot)
    other_edge = lax.ppermute(mate_edge, EVERY, CHIP_MATE)
    far = lax.ppermute(jnp.concatenate([own_edge, other_edge]), EVERY, FAR_MATE)
    mate = lax.ppermute(tile, EVERY, CHIP_MATE)
    next_chip = lax.ppermute(tile, EVERY, NEXT_CHIP)
    far_mate = lax.ppermute(far, EVERY, CHIP_MATE)
    far_next = lax.ppermute(far, EVERY, NEXT_CHIP)
    far_skip = lax.ppermute(far, EVERY, SKIP_CHIP)

    key_spots = np.zeros((2, 8, KEYS), np.float32)
    key_spots[:, :2] = TABLES
    query_spots = np.zeros((2, QUERIES, 8), np.float32)
    query_spots[:, :, :2] = TABLES[:, :, :QUERIES].transpose(0, 2, 1)
    grad_feat, grad_w, scale_tile = pl.pallas_call(
        attention_kernel,
        out_shape=(
            jax.ShapeDtypeStruct((OWN, MODEL), BF16),
            jax.ShapeDtypeStruct((4 * MODEL, MODEL), BF16),
            jax.ShapeDtypeStruct((8, MODEL), BF16),
        ),
        in_specs=[smem, smem] + vmem(12),
        out_specs=vmem(3),
        scratch_shapes=[
            pltpu.VMEM((KEYS, MODEL), BF16),
            pltpu.VMEM((QUERIES, MODEL), BF16),
            pltpu.VMEM((KEYS, MODEL), BF16),
            pltpu.VMEM((KEYS, MODEL), BF16),
            pltpu.VMEM((QUERIES, MODEL), BF16),
            pltpu.VMEM((QUERIES, MODEL), BF16),
            pltpu.VMEM((2, QUERIES, KEYS), F32),
            pltpu.VMEM((2, QUERIES, KEYS), F32),
            pltpu.VMEM((QUERIES, KEYS), F32),
            pltpu.VMEM((2, OWN, NEAR), BF16),
            pltpu.VMEM((2, QUERIES, OWN), BF16),
            pltpu.VMEM((2, OWN, NEAR), BF16),
            pltpu.VMEM((2, QUERIES, OWN), BF16),
        ],
        compiler_params=pltpu.CompilerParams(vmem_limit_bytes=32 * 1024 * 1024),
        name="window_attention",
    )(
        place,
        cos_scale,
        feat,
        cot,
        mate,
        next_chip,
        far,
        far_mate,
        far_next,
        far_skip,
        w_qkv,
        w_out,
        jnp.asarray(key_spots),
        jnp.asarray(query_spots),
    )

    scale_rows = jnp.broadcast_to(scale_tile[None], (SHARES, 8, MODEL))
    shares = jnp.concatenate([grad_w.reshape(SHARES, 16, MODEL), scale_rows], axis=1)
    share = jnp.sum(exchange(shares, PLANES).astype(F32), axis=0)
    pieces = share[16:17, 0:6].reshape(2, 3)
    scale_part = jnp.sum(pieces, axis=1, keepdims=True)
    top = lax.reduce_precision(scale_part, 8, 7)
    middle = lax.reduce_precision(scale_part - top, 8, 7)
    split = jnp.concatenate([top, middle, scale_part - top - middle], axis=1)
    split = jnp.pad(split.reshape(1, 6), ((0, 7), (0, MODEL - 6)))
    share = jnp.concatenate([share[:16], split], axis=0).astype(BF16)
    share = jnp.sum(to_all(share, LINES).astype(F32), axis=0)
    grad_scale = jnp.sum(share[16, 0:6].reshape(2, 3), axis=1)
    whole = to_all(share[:16].astype(BF16), PLANES).astype(F32)
    whole = whole.reshape(4, MODEL, MODEL)
    grad_w_qkv = jnp.concatenate([whole[0], whole[1], whole[2]], axis=1)
    return (grad_feat.reshape(ROWS, COLS, MODEL), grad_w_qkv, whole[3], grad_scale)


def solution(mesh):
    tokens = P("row", "col", None)
    return jax.shard_map(
        on_device,
        mesh=mesh,
        in_specs=(tokens, tokens, P(), P(), P()),
        out_specs=(tokens, P(), P(), P()),
        check_vma=False,
    )
```

```python
import functools

import jax
import jax.numpy as jnp
import numpy as np
from jax import lax
from jax.experimental import pallas as pl
from jax.experimental.pallas import tpu as pltpu
from jax.sharding import PartitionSpec as P

RADIUS = 3
EPSILON = 1e-06
MODEL = 128
HEAD = 64
ROWS, COLS = 8, 16
OWN = ROWS * COLS
QUERIES = 368
KEYS = 640
NEAR = 384
BLOCK = 16
EDGE = 24
SENT = 80
SHARES = 32
LOG2E = 1.4426950408889634
FAR_AWAY = 1e4

F32 = jnp.float32
BF16 = jnp.bfloat16


def side_columns(left, inner):
    if left:
        return -3 if inner else -6
    return 16 if inner else 19


def token_table(core):
    def tile(holder, start, count, lift):
        token = start + np.arange(count)
        return np.stack([8 * holder + token // 16 + lift, token % 16])

    def edge(holder, left, inner, lift):
        token = np.arange(EDGE)
        row = 8 * holder + token // 3 + lift
        return np.stack([row, token % 3 + side_columns(left, inner)])

    other = 1 - core
    lift = -16 if core == 0 else 16
    left = core == 0
    pieces = [
        tile(core, 0, 128, 0),
        tile(other, 80 * core, 48, 0),
        edge(core, left, True, 0),
        edge(other, left, True, 0),
        edge(other, not left, True, 0),
        edge(core, not left, True, 0),
        tile(other, 80 * other, 48, lift),
        edge(other, not left, True, lift),
        edge(other, left, True, lift),
        tile(other, 48 - 16 * core, 48, 0),
        edge(core, left, False, 0),
        edge(other, left, False, 0),
        edge(other, not left, False, 0),
        edge(core, not left, False, 0),
        tile(other, 48 - 16 * other, 48, lift),
        edge(other, not left, False, lift),
        edge(other, left, False, lift),
        np.full((2, 32), FAR_AWAY),
    ]
    return np.concatenate(pieces, axis=1).astype(np.float32)


TABLES = np.stack([token_table(0), token_table(1)])


def vmem(count):
    return [pl.BlockSpec(memory_space=pltpu.VMEM)] * count


def dot_nt(left, right):
    return lax.dot_general(
        left, right, (((1,), (1,)), ((), ())), preferred_element_type=F32
    )


def dot_tn(left, right):
    return lax.dot_general(
        left, right, (((0,), (0,)), ((), ())), preferred_element_type=F32
    )


def dot_nn(left, right):
    return jnp.dot(left, right, preferred_element_type=F32)


def edge_kernel(tile, own_edge, mate_edge):
    core, _, _ = place_here()
    spot = lax.broadcasted_iota(jnp.int32, (SENT, 128), 0)
    token = lax.broadcasted_iota(jnp.int32, (SENT, 128), 1)
    kind = jnp.where(spot >= EDGE, 1, 0) + jnp.where(spot >= 2 * EDGE, 1, 0)
    index = spot - EDGE * kind
    row = (index * 43) >> 7
    step = index - 3 * row
    outer = kind == 1
    right = row * 16 + step + jnp.where(outer, 10, 13)
    left = row * 16 + step + jnp.where(outer, 3, 0)
    used = spot < 3 * EDGE
    from_cot = kind == 2
    for ref, wanted in (
        (own_edge, jnp.where(core == 0, right, left)),
        (mate_edge, jnp.where(core == 0, left, right)),
    ):
        hit = (wanted == token) & used
        of_feat = jnp.where(hit & ~from_cot, 1.0, 0.0).astype(BF16)
        of_cot = jnp.where(hit & from_cot, 1.0, 0.0).astype(BF16)
        ref[...] = (
            dot_nn(of_feat, tile[0:OWN, :]) + dot_nn(of_cot, tile[OWN:, :])
        ).astype(BF16)


def place_here():
    row, col = lax.axis_index("row"), lax.axis_index("col")
    return row & 1, (row >> 1) * 16, col * 16


def rows_at(ref, start, count):
    return ref[pl.ds(pl.multiple_of(start, 16), count), :]


def prepare_kernel(
    cos_scale, tile, _, w_qkv, w_out, key_spots, tile_copy, weights, bias, scales
):
    tile_copy[...] = tile[...]
    head = lax.broadcasted_iota(jnp.int32, (8, KEYS), 0)
    scales[...] = jnp.where(head == 0, cos_scale[0], cos_scale[1])
    for part in range(3):
        columns = slice(part * MODEL, (part + 1) * MODEL)
        weights[columns, :] = w_qkv[:, columns]
    weights[3 * MODEL :, :] = w_out[...]

    core, first_row, first_col = place_here()
    spots = jnp.where(core == 0, key_spots[0], key_spots[1])
    key_rows, key_cols = spots[0:1, :], spots[1:2, :]
    turn = lax.broadcasted_iota(jnp.int32, (16, MODEL), 0)
    turn = jnp.where(turn == lax.broadcasted_iota(jnp.int32, (16, MODEL), 1), 1.0, 0.0)
    query_spots = dot_tn(spots[:, :NEAR].astype(BF16), turn.astype(BF16))
    all_rows = key_rows + first_row.astype(F32)
    all_cols = key_cols + first_col.astype(F32)
    inside = (all_rows >= 0) & (all_rows < 128) & (all_cols >= 0) & (all_cols < 512)
    key_rows = jnp.where(inside, key_rows, FAR_AWAY)
    for start in range(0, QUERIES, BLOCK):
        here = query_spots[start : start + BLOCK, :]
        apart = jnp.maximum(
            jnp.abs(here[:, 0:1] - key_rows), jnp.abs(here[:, 1:2] - key_cols)
        )
        bias[start : start + BLOCK, :] = jnp.where(apart <= RADIUS, 0.0, -1e30)


def attention_kernel(
    scales,
    tile,
    weights,
    mate,
    next_chip,
    far,
    far_skip,
    far_next,
    far_mate,
    bias,
    grad_feat,
    grad_w,
    grad_scale,
    tokens,
    cots,
    keys,
    values,
    queries,
    d_attn,
    raw,
    dots,
    mix_own,
    mix_key,
    slope_own,
    slope_key,
):
    core, _, _ = place_here()
    other = 1 - core
    w_query, w_key, w_value, w_out = (
        weights[start : start + MODEL, :] for start in range(0, 4 * MODEL, MODEL)
    )
    far_wide = far[...].astype(F32)
    mate_wide = far_mate[...].astype(F32)
    next_wide = far_next[0:SENT, :].astype(F32)
    skip_wide = far_skip[SENT:, :].astype(F32)
    edges = (
        far_wide[:SENT],
        far_wide[SENT:],
        mate_wide[:SENT],
        mate_wide[SENT:],
        next_wide,
        skip_wide,
    )

    def strip(kind, chosen):
        pieces = [edge[kind * EDGE : (kind + 1) * EDGE] for edge in chosen]
        return jnp.concatenate(pieces, axis=0).astype(BF16)

    tokens[0:128, :] = tile[0:OWN, :]
    tokens[128:176, :] = rows_at(mate, 80 * core, 48)
    tokens[176:272, :] = strip(0, edges[:4])
    tokens[272:320, :] = rows_at(next_chip, 80 * other, 48)
    tokens[320:368, :] = strip(0, edges[4:])
    tokens[368:416, :] = rows_at(mate, 48 - 16 * core, 48)
    tokens[416:512, :] = strip(1, edges[:4])
    tokens[512:560, :] = rows_at(next_chip, 48 - 16 * other, 48)
    tokens[560:608, :] = strip(1, edges[4:])
    tokens[608:640, :] = jnp.zeros((32, MODEL), BF16)
    cots[0:128, :] = tile[OWN:, :]
    cots[128:176, :] = rows_at(mate, OWN + 80 * core, 48)
    cots[176:272, :] = strip(2, edges[:4])
    cots[272:320, :] = rows_at(next_chip, OWN + 80 * other, 48)
    cots[320:368, :] = strip(2, edges[4:])

    keys[...] = dot_nn(tokens[...], w_key).astype(BF16)
    values[...] = dot_nn(tokens[...], w_value).astype(BF16)
    queries[...] = dot_nn(tokens[0:QUERIES, :], w_query).astype(BF16)
    d_attn[...] = dot_nt(cots[...], w_out).astype(BF16)

    key_wide = keys[...].astype(F32)
    square = key_wide * key_wide
    upper = square.astype(BF16)
    lower = (square - upper.astype(F32)).astype(BF16)
    head_of = lax.broadcasted_iota(jnp.int32, (16, MODEL), 1) // HEAD
    picks = jnp.where(
        head_of == lax.broadcasted_iota(jnp.int32, (16, MODEL), 0), 1.0, 0.0
    ).astype(BF16)
    key_inverse = lax.rsqrt(dot_nt(picks, upper) + dot_nt(picks, lower) + EPSILON)

    first = lax.broadcasted_iota(jnp.int32, (1, MODEL), 1) < HEAD

    def head_sums(array):
        low = jnp.sum(jnp.where(first, array, 0.0), axis=1, keepdims=True)
        high = jnp.sum(jnp.where(first, 0.0, array), axis=1, keepdims=True)
        return low, high

    for head in range(2):
        own_lanes = first if head == 0 else ~first
        raw[head] = dot_nt(jnp.where(own_lanes, queries[...], 0.0).astype(BF16), keys[...])
        dots[head] = dot_nt(jnp.where(own_lanes, d_attn[...], 0.0).astype(BF16), values[...])

    key_inv = [key_inverse[head : head + 1, :] for head in range(2)]
    key_reach = [key_inv[head] * scales[head : head + 1, :] for head in range(2)]
    scale_lanes = jnp.where(first, scales[0:1, :MODEL], scales[1:2, :MODEL])
    scale_sums = [jnp.zeros((BLOCK, 1), F32), jnp.zeros((BLOCK, 1), F32)]
    for start in range(0, QUERIES, BLOCK):
        rows = slice(start, start + BLOCK)
        query_wide = queries[rows, :].astype(F32)
        norms = head_sums(query_wide * query_wide)
        for head in range(2):
            inverse = lax.rsqrt(norms[head] + EPSILON)
            score = raw[head, rows, :] * (inverse * LOG2E) * key_reach[head] + bias[rows, :]
            expo = jnp.exp2(score)
            gain = dots[head, rows, :]
            share = 1.0 / (jnp.sum(expo, axis=1, keepdims=True) + 1e-30)
            center = jnp.sum(expo * gain, axis=1, keepdims=True) * share
            if start < OWN:
                weight = expo[:, :NEAR] * share
                slope = weight * (gain[:, :NEAR] - center)
                pull = slope * key_inv[head][:, :NEAR]
                scale_sums[head] += inverse * jnp.sum(
                    pull * raw[head, rows, :NEAR], axis=1, keepdims=True
                )
                mix_own[head, rows, :] = weight.astype(BF16)
                slope_own[head, rows, :] = pull.astype(BF16)
                weight = weight[:, :OWN]
                slope = slope[:, :OWN]
            else:
                weight = expo[:, :OWN] * share
                slope = weight * (gain[:, :OWN] - center)
            mix_key[head, rows, :] = weight.astype(BF16)
            slope_key[head, rows, :] = (slope * inverse).astype(BF16)

    def both(dot, left, right):
        return jnp.where(first, dot(left[0], right), dot(left[1], right))

    attn_out = both(dot_nn, mix_own, values[0:NEAR, :]).astype(BF16)
    dq_unit = scale_lanes * both(dot_nn, slope_own, keys[0:NEAR, :])
    dk_unit = scale_lanes * both(dot_tn, slope_key, queries[...])
    dv = both(dot_tn, mix_key, d_attn[...])

    def unit_backward(vector, grad_unit):
        low, high = head_sums(vector * vector)
        inverse = jnp.where(first, lax.rsqrt(low + EPSILON), lax.rsqrt(high + EPSILON))
        unit = vector * inverse
        low, high = head_sums(unit * grad_unit)
        return (grad_unit - unit * jnp.where(first, low, high)) * inverse

    dq = unit_backward(queries[0:OWN, :].astype(F32), dq_unit).astype(BF16)
    dk = unit_backward(keys[0:OWN, :].astype(F32), dk_unit).astype(BF16)
    dv = dv.astype(BF16)
    grad_feat[...] = (
        dot_nt(dq, w_query)
        + dot_nt(dk, w_key)
        + dot_nt(dv, w_value)
    ).astype(BF16)
    norm = 1.0 / 256.0
    for part, grad in enumerate((dq, dk, dv)):
        grad_w[part * MODEL : (part + 1) * MODEL, :] = (
            dot_tn(tile[0:OWN, :], grad) * norm
        ).astype(BF16)
    grad_w[3 * MODEL :, :] = (dot_tn(attn_out, tile[OWN:, :]) * norm).astype(BF16)

    lane = lax.broadcasted_iota(jnp.int32, (8, MODEL), 1)
    part = lax.broadcasted_iota(jnp.int32, (8, MODEL), 0)
    terms = [jnp.sum(total, axis=0, keepdims=True) * norm for total in scale_sums]
    rest = jnp.where(lane == 0, terms[0], jnp.where(lane == 1, terms[1], 0.0))
    held = jnp.zeros((8, MODEL), F32)
    for which in range(3):
        piece = rest.astype(BF16).astype(F32)
        held = jnp.where(part == which, piece, held)
        rest = rest - piece
    grad_scale[...] = held.astype(BF16)


def result_kernel(whole, share, grad_w_qkv, grad_w_out, grad_scale):
    for part in range(3):
        rows = slice(part * MODEL, (part + 1) * MODEL)
        grad_w_qkv[:, rows] = whole[rows, :].astype(F32)
    grad_w_out[...] = whole[3 * MODEL :, :].astype(F32)
    total = jnp.sum(share[16:24, :], axis=0, keepdims=True)
    lane = lax.broadcasted_iota(jnp.int32, (1, MODEL), 1)
    for head in range(2):
        grad_scale[head] = jnp.sum(jnp.where(lane == head, total, 0.0))


def pairs(target):
    found = []
    for row in range(16):
        for col in range(32):
            to_row, to_col = target(row, col)
            if 0 <= to_row < 16 and 0 <= to_col < 32:
                found.append((row * 32 + col, to_row * 32 + to_col))
    return found


EVERY = ("row", "col")


def device(x, y, z, core):
    return ((z % 8) * 2 + core) * 32 + (x % 4) * 8 + (y % 4) * 2 + z // 8 % 2


FIRST_X, FIRST_Y, FIRST_Z = 2, 2, 8
PLANES = [
    [
        device(x + FIRST_X, y + FIRST_Y, z, core)
        for x in range(4)
        for y in range(4)
        for core in range(2)
    ]
    for z in range(16)
]
LINES = [
    [device(x, y, z + FIRST_Z, core) for z in range(16)]
    for x in range(4)
    for y in range(4)
    for core in range(2)
]
CHIP_MATE = pairs(lambda row, col: (row ^ 1, col))
FAR_MATE = pairs(lambda row, col: (row, col - 1 if row % 2 else col + 1))
NEXT_CHIP = pairs(lambda row, col: (row + 1 if row % 2 else row - 1, col))
SKIP_CHIP = pairs(lambda row, col: (row - 2 if row % 2 else row + 2, col))


def exchange(array, groups):
    return lax.all_to_all(array, EVERY, 0, 0, axis_index_groups=groups, tiled=True)


def to_all(array, groups):
    return exchange(jnp.broadcast_to(array[None], (len(groups[0]),) + array.shape), groups)


def on_device(features, cotangent, w_qkv, w_out, cos_scale):
    feat = features.reshape(OWN, MODEL)
    cot = cotangent.reshape(OWN, MODEL)
    smem = pl.BlockSpec(memory_space=pltpu.SMEM)

    edge = jax.ShapeDtypeStruct((SENT, MODEL), BF16)
    tile = jnp.concatenate([feat, cot])
    own_edge, mate_edge = pl.pallas_call(
        edge_kernel,
        out_shape=(edge, edge),
        in_specs=vmem(1),
        out_specs=vmem(2),
        compiler_params=pltpu.CompilerParams(vmem_limit_bytes=2 * 1024 * 1024),
        name="edges",
    )(tile)
    other_edge = lax.ppermute(mate_edge, EVERY, CHIP_MATE)
    far = lax.ppermute(jnp.concatenate([own_edge, other_edge]), EVERY, FAR_MATE)
    key_spots = np.zeros((2, 16, KEYS), np.float32)
    key_spots[:, :2] = TABLES
    key_spots = jnp.asarray(key_spots)
    tile_copy, weights, bias, scales = pl.pallas_call(
        prepare_kernel,
        out_shape=(
            jax.ShapeDtypeStruct((2 * OWN, MODEL), BF16),
            jax.ShapeDtypeStruct((4 * MODEL, MODEL), BF16),
            jax.ShapeDtypeStruct((QUERIES, KEYS), F32),
            jax.ShapeDtypeStruct((8, KEYS), F32),
        ),
        in_specs=[smem] + vmem(5),
        out_specs=vmem(4),
        compiler_params=pltpu.CompilerParams(vmem_limit_bytes=4 * 1024 * 1024),
        cost_estimate=pl.CostEstimate(
            flops=1000000, bytes_accessed=1 << 20, transcendentals=0
        ),
        name="prepare",
    )(cos_scale, tile, other_edge, w_qkv, w_out, key_spots)
    mate = lax.ppermute(tile_copy, EVERY, CHIP_MATE)
    next_chip = lax.ppermute(tile_copy, EVERY, NEXT_CHIP)

    far_mate = lax.ppermute(far, EVERY, CHIP_MATE)
    far_next = lax.ppermute(far, EVERY, NEXT_CHIP)
    far_skip = lax.ppermute(far, EVERY, SKIP_CHIP)
    grad_feat, grad_w, scale_tile = pl.pallas_call(
        attention_kernel,
        out_shape=(
            jax.ShapeDtypeStruct((OWN, MODEL), BF16),
            jax.ShapeDtypeStruct((4 * MODEL, MODEL), BF16),
            jax.ShapeDtypeStruct((8, MODEL), BF16),
        ),
        in_specs=vmem(10),
        out_specs=vmem(3),
        scratch_shapes=[
            pltpu.VMEM((KEYS, MODEL), BF16),
            pltpu.VMEM((QUERIES, MODEL), BF16),
            pltpu.VMEM((KEYS, MODEL), BF16),
            pltpu.VMEM((KEYS, MODEL), BF16),
            pltpu.VMEM((QUERIES, MODEL), BF16),
            pltpu.VMEM((QUERIES, MODEL), BF16),
            pltpu.VMEM((2, QUERIES, KEYS), F32),
            pltpu.VMEM((2, QUERIES, KEYS), F32),
            pltpu.VMEM((2, OWN, NEAR), BF16),
            pltpu.VMEM((2, QUERIES, OWN), BF16),
            pltpu.VMEM((2, OWN, NEAR), BF16),
            pltpu.VMEM((2, QUERIES, OWN), BF16),
        ],
        compiler_params=pltpu.CompilerParams(vmem_limit_bytes=16 * 1024 * 1024),
        name="window_attention",
    )(
        scales,
        tile,
        weights,
        mate,
        next_chip,
        far,
        far_skip,
        far_next,
        far_mate,
        bias,
    )

    scale_rows = jnp.broadcast_to(scale_tile[None], (SHARES, 8, MODEL))
    shares = jnp.concatenate([grad_w.reshape(SHARES, 16, MODEL), scale_rows], axis=1)
    share = jnp.sum(exchange(shares, PLANES).astype(F32), axis=0)
    scale_row = jnp.sum(share[16:19], axis=0, keepdims=True)
    top = lax.reduce_precision(scale_row, 8, 7)
    middle = lax.reduce_precision(scale_row - top, 8, 7)
    split = [share[:16], top, middle, scale_row - top - middle, jnp.zeros((5, MODEL), F32)]
    share = jnp.concatenate(split, axis=0).astype(BF16)
    share = jnp.sum(to_all(share, LINES).astype(F32), axis=0)
    whole = to_all(share[:16].astype(BF16), PLANES).reshape(4 * MODEL, MODEL)
    grad_w_qkv, grad_w_out, grad_scale = pl.pallas_call(
        result_kernel,
        out_shape=(
            jax.ShapeDtypeStruct((MODEL, 3 * MODEL), F32),
            jax.ShapeDtypeStruct((MODEL, MODEL), F32),
            jax.ShapeDtypeStruct((2,), F32),
        ),
        in_specs=vmem(2),
        out_specs=vmem(2) + [smem],
        compiler_params=pltpu.CompilerParams(vmem_limit_bytes=2 * 1024 * 1024),
        name="results",
    )(whole, share)
    return (grad_feat.reshape(ROWS, COLS, MODEL), grad_w_qkv, grad_w_out, grad_scale)


def solution(mesh):
    tokens = P("row", "col", None)
    return jax.shard_map(
        on_device,
        mesh=mesh,
        in_specs=(tokens, tokens, P(), P(), P()),
        out_specs=(tokens, P(), P(), P()),
        check_vma=False,
    )
```

```python
import functools

import jax
import jax.numpy as jnp
import numpy as np
from jax import lax
from jax.experimental import pallas as pl
from jax.experimental.pallas import tpu as pltpu
from jax.sharding import PartitionSpec as P

RADIUS = 3
EPSILON = 1e-06
MODEL = 128
HEAD = 64
ROWS, COLS = 8, 16
OWN = ROWS * COLS
QUERIES = 368
KEYS = 640
NEAR = 384
BLOCK = 16
EDGE = 24
SENT = 80
SHARES = 32
LOG2E = 1.4426950408889634
FAR_AWAY = 1e4

F32 = jnp.float32
BF16 = jnp.bfloat16


def side_columns(left, inner):
    if left:
        return -3 if inner else -6
    return 16 if inner else 19


def token_table(core):
    def tile(holder, start, count, lift):
        token = start + np.arange(count)
        return np.stack([8 * holder + token // 16 + lift, token % 16])

    def edge(holder, left, inner, lift):
        token = np.arange(EDGE)
        row = 8 * holder + token // 3 + lift
        return np.stack([row, token % 3 + side_columns(left, inner)])

    other = 1 - core
    lift = -16 if core == 0 else 16
    left = core == 0
    pieces = [
        tile(core, 0, 128, 0),
        tile(other, 80 * core, 48, 0),
        edge(core, left, True, 0),
        edge(other, left, True, 0),
        edge(other, not left, True, 0),
        edge(core, not left, True, 0),
        tile(other, 80 * other, 48, lift),
        edge(other, not left, True, lift),
        edge(other, left, True, lift),
        tile(other, 48 - 16 * core, 48, 0),
        edge(core, left, False, 0),
        edge(other, left, False, 0),
        edge(other, not left, False, 0),
        edge(core, not left, False, 0),
        tile(other, 48 - 16 * other, 48, lift),
        edge(other, not left, False, lift),
        edge(other, left, False, lift),
        np.full((2, 32), FAR_AWAY),
    ]
    return np.concatenate(pieces, axis=1).astype(np.float32)


TABLES = np.stack([token_table(0), token_table(1)])


def vmem(count):
    return [pl.BlockSpec(memory_space=pltpu.VMEM)] * count


def dot_nt(left, right):
    return lax.dot_general(
        left, right, (((1,), (1,)), ((), ())), preferred_element_type=F32
    )


def dot_tn(left, right):
    return lax.dot_general(
        left, right, (((0,), (0,)), ((), ())), preferred_element_type=F32
    )


def dot_nn(left, right):
    return jnp.dot(left, right, preferred_element_type=F32)


def edge_kernel(tile, own_edge, mate_message):
    core, _, _ = place_here()
    spot = lax.broadcasted_iota(jnp.int32, (SENT, 128), 0)
    token = lax.broadcasted_iota(jnp.int32, (SENT, 128), 1)
    kind = jnp.where(spot >= EDGE, 1, 0) + jnp.where(spot >= 2 * EDGE, 1, 0)
    index = spot - EDGE * kind
    row = (index * 43) >> 7
    step = index - 3 * row
    outer = kind == 1
    right = row * 16 + step + jnp.where(outer, 10, 13)
    left = row * 16 + step + jnp.where(outer, 3, 0)
    used = spot < 3 * EDGE
    from_cot = kind == 2
    for ref, wanted in (
        (own_edge, jnp.where(core == 0, right, left)),
        (mate_message, jnp.where(core == 0, left, right)),
    ):
        hit = (wanted == token) & used
        of_feat = jnp.where(hit & ~from_cot, 1.0, 0.0).astype(BF16)
        of_cot = jnp.where(hit & from_cot, 1.0, 0.0).astype(BF16)
        ref[0:SENT, :] = (
            dot_nn(of_feat, tile[0:OWN, :]) + dot_nn(of_cot, tile[OWN:, :])
        ).astype(BF16)
    half = 1 - core
    mate_message[SENT : SENT + 48, :] = rows_at(tile, 80 * half, 48)
    mate_message[SENT + 48 : SENT + 96, :] = rows_at(tile, 48 - 16 * half, 48)
    mate_message[SENT + 96 : SENT + 144, :] = rows_at(tile, OWN + 80 * half, 48)


def place_here():
    row, col = lax.axis_index("row"), lax.axis_index("col")
    return row & 1, (row >> 1) * 16, col * 16


def rows_at(ref, start, count):
    return ref[pl.ds(pl.multiple_of(start, 16), count), :]


def prepare_kernel(tile, _, w_qkv, w_out, key_spots, tile_copy, weights, bias):
    tile_copy[...] = tile[...]
    for part in range(3):
        columns = slice(part * MODEL, (part + 1) * MODEL)
        weights[columns, :] = w_qkv[:, columns]
    weights[3 * MODEL :, :] = w_out[...]

    core, first_row, first_col = place_here()
    spots = jnp.where(core == 0, key_spots[0], key_spots[1])
    key_rows, key_cols = spots[0:1, :], spots[1:2, :]
    turn = lax.broadcasted_iota(jnp.int32, (16, MODEL), 0)
    turn = jnp.where(turn == lax.broadcasted_iota(jnp.int32, (16, MODEL), 1), 1.0, 0.0)
    query_spots = dot_tn(spots[:, :NEAR].astype(BF16), turn.astype(BF16))
    all_rows = key_rows + first_row.astype(F32)
    all_cols = key_cols + first_col.astype(F32)
    inside = (all_rows >= 0) & (all_rows < 128) & (all_cols >= 0) & (all_cols < 512)
    key_rows = jnp.where(inside, key_rows, FAR_AWAY)
    for start in range(0, QUERIES, BLOCK):
        here = query_spots[start : start + BLOCK, :]
        apart = jnp.maximum(
            jnp.abs(here[:, 0:1] - key_rows), jnp.abs(here[:, 1:2] - key_cols)
        )
        bias[start : start + BLOCK, :] = jnp.where(apart <= RADIUS, 0.0, -1e30)


def attention_kernel(
    scales,
    tile,
    weights,
    mate,
    next_chip,
    far,
    far_skip,
    far_next,
    far_mate,
    bias,
    grad_feat,
    grad_w,
    grad_scale,
    tokens,
    cots,
    keys,
    values,
    queries,
    d_attn,
    raw,
    dots,
    mix_own,
    mix_key,
    slope_own,
    slope_key,
):
    core, _, _ = place_here()
    other = 1 - core
    w_query, w_key, w_value, w_out = (
        weights[start : start + MODEL, :] for start in range(0, 4 * MODEL, MODEL)
    )
    far_wide = far[...].astype(F32)
    mate_wide = far_mate[...].astype(F32)
    next_wide = far_next[0:SENT, :].astype(F32)
    skip_wide = far_skip[SENT:, :].astype(F32)
    edges = (
        far_wide[:SENT],
        far_wide[SENT:],
        mate_wide[:SENT],
        mate_wide[SENT:],
        next_wide,
        skip_wide,
    )

    def strip(kind, chosen):
        pieces = [edge[kind * EDGE : (kind + 1) * EDGE] for edge in chosen]
        return jnp.concatenate(pieces, axis=0).astype(BF16)

    tokens[0:128, :] = tile[0:OWN, :]
    tokens[128:176, :] = mate[SENT : SENT + 48, :]
    tokens[176:272, :] = strip(0, edges[:4])
    tokens[272:320, :] = rows_at(next_chip, 80 * other, 48)
    tokens[320:368, :] = strip(0, edges[4:])
    tokens[368:416, :] = mate[SENT + 48 : SENT + 96, :]
    tokens[416:512, :] = strip(1, edges[:4])
    tokens[512:560, :] = rows_at(next_chip, 48 - 16 * other, 48)
    tokens[560:608, :] = strip(1, edges[4:])
    tokens[608:640, :] = jnp.zeros((32, MODEL), BF16)
    cots[0:128, :] = tile[OWN:, :]
    cots[128:176, :] = mate[SENT + 96 : SENT + 144, :]
    cots[176:272, :] = strip(2, edges[:4])
    cots[272:320, :] = rows_at(next_chip, OWN + 80 * other, 48)
    cots[320:368, :] = strip(2, edges[4:])

    keys[...] = dot_nn(tokens[...], w_key).astype(BF16)
    values[...] = dot_nn(tokens[...], w_value).astype(BF16)
    queries[...] = dot_nn(tokens[0:QUERIES, :], w_query).astype(BF16)
    d_attn[...] = dot_nt(cots[...], w_out).astype(BF16)

    key_wide = keys[...].astype(F32)
    square = key_wide * key_wide
    upper = square.astype(BF16)
    lower = (square - upper.astype(F32)).astype(BF16)
    head_of = lax.broadcasted_iota(jnp.int32, (16, MODEL), 1) // HEAD
    picks = jnp.where(
        head_of == lax.broadcasted_iota(jnp.int32, (16, MODEL), 0), 1.0, 0.0
    ).astype(BF16)
    key_inverse = lax.rsqrt(dot_nt(picks, upper) + dot_nt(picks, lower) + EPSILON)

    first = lax.broadcasted_iota(jnp.int32, (1, MODEL), 1) < HEAD

    def head_sums(array):
        low = jnp.sum(jnp.where(first, array, 0.0), axis=1, keepdims=True)
        high = jnp.sum(jnp.where(first, 0.0, array), axis=1, keepdims=True)
        return low, high

    for head in range(2):
        own_lanes = first if head == 0 else ~first
        raw[head] = dot_nt(jnp.where(own_lanes, queries[...], 0.0).astype(BF16), keys[...])
        dots[head] = dot_nt(jnp.where(own_lanes, d_attn[...], 0.0).astype(BF16), values[...])

    key_inv = [key_inverse[head : head + 1, :] for head in range(2)]
    key_reach = [key_inv[head] * scales[head : head + 1, :] for head in range(2)]
    scale_lanes = jnp.where(first, scales[0:1, :MODEL], scales[1:2, :MODEL])
    scale_sums = [jnp.zeros((BLOCK, 1), F32), jnp.zeros((BLOCK, 1), F32)]
    for start in range(0, QUERIES, BLOCK):
        rows = slice(start, start + BLOCK)
        query_wide = queries[rows, :].astype(F32)
        norms = head_sums(query_wide * query_wide)
        for head in range(2):
            inverse = lax.rsqrt(norms[head] + EPSILON)
            score = raw[head, rows, :] * (inverse * LOG2E) * key_reach[head] + bias[rows, :]
            expo = jnp.exp2(score)
            gain = dots[head, rows, :]
            share = 1.0 / (jnp.sum(expo, axis=1, keepdims=True) + 1e-30)
            center = jnp.sum(expo * gain, axis=1, keepdims=True) * share
            if start < OWN:
                weight = expo[:, :NEAR] * share
                slope = weight * (gain[:, :NEAR] - center)
                pull = slope * key_inv[head][:, :NEAR]
                scale_sums[head] += inverse * jnp.sum(
                    pull * raw[head, rows, :NEAR], axis=1, keepdims=True
                )
                mix_own[head, rows, :] = weight.astype(BF16)
                slope_own[head, rows, :] = pull.astype(BF16)
                weight = weight[:, :OWN]
                slope = slope[:, :OWN]
            else:
                weight = expo[:, :OWN] * share
                slope = weight * (gain[:, :OWN] - center)
            mix_key[head, rows, :] = weight.astype(BF16)
            slope_key[head, rows, :] = (slope * inverse).astype(BF16)

    def both(dot, left, right):
        return jnp.where(first, dot(left[0], right), dot(left[1], right))

    attn_out = both(dot_nn, mix_own, values[0:NEAR, :]).astype(BF16)
    dq_unit = scale_lanes * both(dot_nn, slope_own, keys[0:NEAR, :])
    dk_unit = scale_lanes * both(dot_tn, slope_key, queries[...])
    dv = both(dot_tn, mix_key, d_attn[...])

    def unit_backward(vector, grad_unit):
        low, high = head_sums(vector * vector)
        inverse = jnp.where(first, lax.rsqrt(low + EPSILON), lax.rsqrt(high + EPSILON))
        unit = vector * inverse
        low, high = head_sums(unit * grad_unit)
        return (grad_unit - unit * jnp.where(first, low, high)) * inverse

    dq = unit_backward(queries[0:OWN, :].astype(F32), dq_unit).astype(BF16)
    dk = unit_backward(keys[0:OWN, :].astype(F32), dk_unit).astype(BF16)
    dv = dv.astype(BF16)
    grad_feat[...] = (
        dot_nt(dq, w_query)
        + dot_nt(dk, w_key)
        + dot_nt(dv, w_value)
    ).astype(BF16)
    norm = 1.0 / 256.0
    for part, grad in enumerate((dq, dk, dv)):
        grad_w[part * MODEL : (part + 1) * MODEL, :] = (
            dot_tn(tile[0:OWN, :], grad) * norm
        ).astype(BF16)
    grad_w[3 * MODEL :, :] = (dot_tn(attn_out, tile[OWN:, :]) * norm).astype(BF16)

    lane = lax.broadcasted_iota(jnp.int32, (8, MODEL), 1)
    part = lax.broadcasted_iota(jnp.int32, (8, MODEL), 0)
    terms = [jnp.sum(total, axis=0, keepdims=True) * norm for total in scale_sums]
    rest = jnp.where(part == 0, terms[0], terms[1])
    held = jnp.zeros((8, MODEL), F32)
    for which in range(3):
        piece = rest.astype(BF16).astype(F32)
        held = jnp.where(lane == which, piece, held)
        rest = rest - piece
    grad_scale[...] = held.astype(BF16)


def result_kernel(whole, terms, feat_tile, grad_feat, grad_w_qkv, grad_w_out, grad_scale):
    grad_feat[...] = feat_tile[...]
    for part in range(3):
        rows = slice(part * MODEL, (part + 1) * MODEL)
        grad_w_qkv[:, rows] = whole[rows, :].astype(F32)
    grad_w_out[...] = whole[3 * MODEL :, :].astype(F32)
    for head in range(2):
        grad_scale[head] = jnp.sum(terms[head : head + 1, :])


def pairs(target):
    found = []
    for row in range(16):
        for col in range(32):
            to_row, to_col = target(row, col)
            if 0 <= to_row < 16 and 0 <= to_col < 32:
                found.append((row * 32 + col, to_row * 32 + to_col))
    return found


EVERY = ("row", "col")


def device(x, y, z, core):
    return ((z % 8) * 2 + core) * 32 + (x % 4) * 8 + (y % 4) * 2 + z // 8 % 2


FIRST_X, FIRST_Y, FIRST_Z = 2, 2, 9
PLANES = [
    [
        device(x + FIRST_X, y + FIRST_Y, z, core)
        for x in range(4)
        for y in range(4)
        for core in range(2)
    ]
    for z in range(16)
]
LINES = [
    [device(x, y, z + FIRST_Z, core) for z in range(16)]
    for x in range(4)
    for y in range(4)
    for core in range(2)
]
CHIP_MATE = pairs(lambda row, col: (row ^ 1, col))
FAR_MATE = pairs(lambda row, col: (row, col - 1 if row % 2 else col + 1))
NEXT_CHIP = pairs(lambda row, col: (row + 1 if row % 2 else row - 1, col))
SKIP_CHIP = pairs(lambda row, col: (row - 2 if row % 2 else row + 2, col))


def exchange(array, groups):
    return lax.all_to_all(array, EVERY, 0, 0, axis_index_groups=groups, tiled=True)


def to_all(array, groups):
    return exchange(jnp.broadcast_to(array[None], (len(groups[0]),) + array.shape), groups)


def on_device(features, cotangent, w_qkv, w_out, cos_scale):
    feat = features.reshape(OWN, MODEL)
    cot = cotangent.reshape(OWN, MODEL)
    smem = pl.BlockSpec(memory_space=pltpu.SMEM)

    edge = jax.ShapeDtypeStruct((SENT, MODEL), BF16)
    tile = jnp.concatenate([feat, cot])
    own_edge, mate_message = pl.pallas_call(
        edge_kernel,
        out_shape=(edge, jax.ShapeDtypeStruct((SENT + 144, MODEL), BF16)),
        in_specs=vmem(1),
        out_specs=vmem(2),
        compiler_params=pltpu.CompilerParams(vmem_limit_bytes=2 * 1024 * 1024),
        name="edges",
    )(tile)
    mate = lax.ppermute(mate_message, EVERY, CHIP_MATE)
    other_edge = mate[:SENT]
    far = lax.ppermute(jnp.concatenate([own_edge, other_edge]), EVERY, FAR_MATE)
    key_spots = np.zeros((2, 16, KEYS), np.float32)
    key_spots[:, :2] = TABLES
    key_spots = jnp.asarray(key_spots)
    scales = jnp.broadcast_to(cos_scale[None, :, None], (4, 2, KEYS)).reshape(8, KEYS)
    tile_copy, weights, bias = pl.pallas_call(
        prepare_kernel,
        out_shape=(
            jax.ShapeDtypeStruct((2 * OWN, MODEL), BF16),
            jax.ShapeDtypeStruct((4 * MODEL, MODEL), BF16),
            jax.ShapeDtypeStruct((QUERIES, KEYS), F32),
        ),
        in_specs=vmem(5),
        out_specs=vmem(3),
        compiler_params=pltpu.CompilerParams(vmem_limit_bytes=4 * 1024 * 1024),
        cost_estimate=pl.CostEstimate(
            flops=1000000, bytes_accessed=1 << 20, transcendentals=0
        ),
        name="prepare",
    )(tile, mate, w_qkv, w_out, key_spots)
    next_chip = lax.ppermute(tile_copy, EVERY, NEXT_CHIP)

    far_mate = lax.ppermute(far, EVERY, CHIP_MATE)
    far_next = lax.ppermute(far, EVERY, NEXT_CHIP)
    far_skip = lax.ppermute(far, EVERY, SKIP_CHIP)
    grad_feat, grad_w, scale_tile = pl.pallas_call(
        attention_kernel,
        out_shape=(
            jax.ShapeDtypeStruct((OWN, MODEL), BF16),
            jax.ShapeDtypeStruct((4 * MODEL, MODEL), BF16),
            jax.ShapeDtypeStruct((8, MODEL), BF16),
        ),
        in_specs=vmem(10),
        out_specs=vmem(3),
        scratch_shapes=[
            pltpu.VMEM((KEYS, MODEL), BF16),
            pltpu.VMEM((QUERIES, MODEL), BF16),
            pltpu.VMEM((KEYS, MODEL), BF16),
            pltpu.VMEM((KEYS, MODEL), BF16),
            pltpu.VMEM((QUERIES, MODEL), BF16),
            pltpu.VMEM((QUERIES, MODEL), BF16),
            pltpu.VMEM((2, QUERIES, KEYS), F32),
            pltpu.VMEM((2, QUERIES, KEYS), F32),
            pltpu.VMEM((2, OWN, NEAR), BF16),
            pltpu.VMEM((2, QUERIES, OWN), BF16),
            pltpu.VMEM((2, OWN, NEAR), BF16),
            pltpu.VMEM((2, QUERIES, OWN), BF16),
        ],
        compiler_params=pltpu.CompilerParams(vmem_limit_bytes=16 * 1024 * 1024),
        name="window_attention",
    )(
        scales,
        tile,
        weights,
        mate,
        next_chip,
        far,
        far_skip,
        far_next,
        far_mate,
        bias,
    )

    scale_rows = jnp.broadcast_to(scale_tile[None, None, :2], (SHARES, 1, 2, MODEL))
    shares = jnp.concatenate([grad_w.reshape(SHARES, 8, 2, MODEL), scale_rows], axis=1)
    lane = lax.broadcasted_iota(jnp.int32, (2, MODEL), 1)
    shares, lane = lax.optimization_barrier((shares, lane))
    share = jnp.sum(exchange(shares, PLANES).astype(F32), axis=0)
    term = jnp.sum(jnp.where(lane < 3, share[8], 0.0), axis=1, keepdims=True)
    top = lax.reduce_precision(term, 8, 7)
    middle = lax.reduce_precision(term - top, 8, 7)
    parts = jnp.where(lane == 0, top, jnp.where(lane == 1, middle, term - top - middle))
    parts = jnp.where(lane < 3, parts, 0.0)
    share = jnp.concatenate([share[:8], parts[None]], axis=0).astype(BF16)
    share = jnp.sum(to_all(share, LINES).astype(F32), axis=0)
    share, terms = lax.optimization_barrier((share[:8].astype(BF16).reshape(16, MODEL), share[8]))
    whole = to_all(share, PLANES).reshape(4 * MODEL, MODEL)
    grad_feat, grad_w_qkv, grad_w_out, grad_scale = pl.pallas_call(
        result_kernel,
        out_shape=(
            jax.ShapeDtypeStruct((OWN, MODEL), BF16),
            jax.ShapeDtypeStruct((MODEL, 3 * MODEL), F32),
            jax.ShapeDtypeStruct((MODEL, MODEL), F32),
            jax.ShapeDtypeStruct((2,), F32),
        ),
        in_specs=vmem(3),
        out_specs=vmem(3) + [smem],
        compiler_params=pltpu.CompilerParams(vmem_limit_bytes=2 * 1024 * 1024),
        name="results",
    )(whole, terms, grad_feat)
    return (grad_feat.reshape(ROWS, COLS, MODEL), grad_w_qkv, grad_w_out, grad_scale)


def solution(mesh):
    tokens = P("row", "col", None)
    return jax.shard_map(
        on_device,
        mesh=mesh,
        in_specs=(tokens, tokens, P(), P(), P()),
        out_specs=(tokens, P(), P(), P()),
        check_vma=False,
    )
```

```python
import functools

import jax
import jax.numpy as jnp
import numpy as np
from jax import lax
from jax.experimental import pallas as pl
from jax.experimental.pallas import tpu as pltpu
from jax.sharding import PartitionSpec as P

RADIUS = 3
EPSILON = 1e-06
MODEL = 128
HEAD = 64
ROWS, COLS = 8, 16
OWN = ROWS * COLS
QUERIES = 368
KEYS = 640
NEAR = 384
BLOCK = 16
EDGE = 24
SENT = 80
SHARES = 32
LOG2E = 1.4426950408889634
FAR_AWAY = 1e4

F32 = jnp.float32
BF16 = jnp.bfloat16


def side_columns(left, inner):
    if left:
        return -3 if inner else -6
    return 16 if inner else 19


def token_table(core):
    def tile(holder, start, count, lift):
        token = start + np.arange(count)
        return np.stack([8 * holder + token // 16 + lift, token % 16])

    def edge(holder, left, inner, lift):
        token = np.arange(EDGE)
        row = 8 * holder + token // 3 + lift
        return np.stack([row, token % 3 + side_columns(left, inner)])

    other = 1 - core
    lift = -16 if core == 0 else 16
    left = core == 0
    pieces = [
        tile(core, 0, 128, 0),
        tile(other, 80 * core, 48, 0),
        edge(core, left, True, 0),
        edge(other, left, True, 0),
        edge(other, not left, True, 0),
        edge(core, not left, True, 0),
        tile(other, 80 * other, 48, lift),
        edge(other, not left, True, lift),
        edge(other, left, True, lift),
        tile(other, 48 - 16 * core, 48, 0),
        edge(core, left, False, 0),
        edge(other, left, False, 0),
        edge(other, not left, False, 0),
        edge(core, not left, False, 0),
        tile(other, 48 - 16 * other, 48, lift),
        edge(other, not left, False, lift),
        edge(other, left, False, lift),
        np.full((2, 32), FAR_AWAY),
    ]
    return np.concatenate(pieces, axis=1).astype(np.float32)


TABLES = np.stack([token_table(0), token_table(1)])


def vmem(count):
    return [pl.BlockSpec(memory_space=pltpu.VMEM)] * count


def dot_nt(left, right):
    return lax.dot_general(
        left, right, (((1,), (1,)), ((), ())), preferred_element_type=F32
    )


def dot_tn(left, right):
    return lax.dot_general(
        left, right, (((0,), (0,)), ((), ())), preferred_element_type=F32
    )


def dot_nn(left, right):
    return jnp.dot(left, right, preferred_element_type=F32)


def edge_kernel(tile, own_edge, mate_message):
    core, _, _ = place_here()
    spot = lax.broadcasted_iota(jnp.int32, (SENT, 128), 0)
    token = lax.broadcasted_iota(jnp.int32, (SENT, 128), 1)
    kind = jnp.where(spot >= EDGE, 1, 0) + jnp.where(spot >= 2 * EDGE, 1, 0)
    index = spot - EDGE * kind
    row = (index * 43) >> 7
    step = index - 3 * row
    outer = kind == 1
    right = row * 16 + step + jnp.where(outer, 10, 13)
    left = row * 16 + step + jnp.where(outer, 3, 0)
    used = spot < 3 * EDGE
    from_cot = kind == 2
    for ref, wanted in (
        (own_edge, jnp.where(core == 0, right, left)),
        (mate_message, jnp.where(core == 0, left, right)),
    ):
        hit = (wanted == token) & used
        of_feat = jnp.where(hit & ~from_cot, 1.0, 0.0).astype(BF16)
        of_cot = jnp.where(hit & from_cot, 1.0, 0.0).astype(BF16)
        ref[0:SENT, :] = (
            dot_nn(of_feat, tile[0:OWN, :]) + dot_nn(of_cot, tile[OWN:, :])
        ).astype(BF16)
    half = 1 - core
    mate_message[SENT : SENT + 48, :] = rows_at(tile, 80 * half, 48)
    mate_message[SENT + 48 : SENT + 96, :] = rows_at(tile, 48 - 16 * half, 48)
    mate_message[SENT + 96 : SENT + 144, :] = rows_at(tile, OWN + 80 * half, 48)


def place_here():
    row, col = lax.axis_index("row"), lax.axis_index("col")
    return row & 1, (row >> 1) * 16, col * 16


def rows_at(ref, start, count):
    return ref[pl.ds(pl.multiple_of(start, 16), count), :]


def prepare_kernel(tile, _, w_qkv, w_out, key_spots, tile_copy, weights, bias):
    tile_copy[...] = tile[...]
    for part in range(3):
        columns = slice(part * MODEL, (part + 1) * MODEL)
        weights[columns, :] = w_qkv[:, columns]
    weights[3 * MODEL :, :] = w_out[...]

    core, first_row, first_col = place_here()
    spots = jnp.where(core == 0, key_spots[0], key_spots[1])
    key_rows, key_cols = spots[0:1, :], spots[1:2, :]
    turn = lax.broadcasted_iota(jnp.int32, (16, MODEL), 0)
    turn = jnp.where(turn == lax.broadcasted_iota(jnp.int32, (16, MODEL), 1), 1.0, 0.0)
    query_spots = dot_tn(spots[:, :NEAR].astype(BF16), turn.astype(BF16))
    all_rows = key_rows + first_row.astype(F32)
    all_cols = key_cols + first_col.astype(F32)
    inside = (all_rows >= 0) & (all_rows < 128) & (all_cols >= 0) & (all_cols < 512)
    key_rows = jnp.where(inside, key_rows, FAR_AWAY)
    for start in range(0, QUERIES, BLOCK):
        here = query_spots[start : start + BLOCK, :]
        apart = jnp.maximum(
            jnp.abs(here[:, 0:1] - key_rows), jnp.abs(here[:, 1:2] - key_cols)
        )
        bias[start : start + BLOCK, :] = jnp.where(apart <= RADIUS, 0.0, -1e30)


def attention_kernel(
    scales,
    tile,
    weights,
    mate,
    next_chip,
    far,
    far_skip,
    far_next,
    far_mate,
    bias,
    grad_feat,
    grad_w,
    grad_scale,
    tokens,
    cots,
    keys,
    values,
    queries,
    d_attn,
    raw,
    dots,
    mix_own,
    mix_key,
    slope_own,
    slope_key,
):
    core, _, _ = place_here()
    other = 1 - core
    w_query, w_key, w_value, w_out = (
        weights[start : start + MODEL, :] for start in range(0, 4 * MODEL, MODEL)
    )
    far_wide = far[...].astype(F32)
    mate_wide = far_mate[...].astype(F32)
    next_wide = far_next[0:SENT, :].astype(F32)
    skip_wide = far_skip[SENT:, :].astype(F32)
    edges = (
        far_wide[:SENT],
        far_wide[SENT:],
        mate_wide[:SENT],
        mate_wide[SENT:],
        next_wide,
        skip_wide,
    )

    def strip(kind, chosen):
        pieces = [edge[kind * EDGE : (kind + 1) * EDGE] for edge in chosen]
        return jnp.concatenate(pieces, axis=0).astype(BF16)

    tokens[0:128, :] = tile[0:OWN, :]
    tokens[128:176, :] = mate[SENT : SENT + 48, :]
    tokens[176:272, :] = strip(0, edges[:4])
    tokens[272:320, :] = rows_at(next_chip, 80 * other, 48)
    tokens[320:368, :] = strip(0, edges[4:])
    tokens[368:416, :] = mate[SENT + 48 : SENT + 96, :]
    tokens[416:512, :] = strip(1, edges[:4])
    tokens[512:560, :] = rows_at(next_chip, 48 - 16 * other, 48)
    tokens[560:608, :] = strip(1, edges[4:])
    tokens[608:640, :] = jnp.zeros((32, MODEL), BF16)
    cots[0:128, :] = tile[OWN:, :]
    cots[128:176, :] = mate[SENT + 96 : SENT + 144, :]
    cots[176:272, :] = strip(2, edges[:4])
    cots[272:320, :] = rows_at(next_chip, OWN + 80 * other, 48)
    cots[320:368, :] = strip(2, edges[4:])

    keys[...] = dot_nn(tokens[...], w_key).astype(BF16)
    values[...] = dot_nn(tokens[...], w_value).astype(BF16)
    queries[...] = dot_nn(tokens[0:QUERIES, :], w_query).astype(BF16)
    d_attn[...] = dot_nt(cots[...], w_out).astype(BF16)

    key_wide = keys[...].astype(F32)
    square = key_wide * key_wide
    upper = square.astype(BF16)
    lower = (square - upper.astype(F32)).astype(BF16)
    head_of = lax.broadcasted_iota(jnp.int32, (16, MODEL), 1) // HEAD
    picks = jnp.where(
        head_of == lax.broadcasted_iota(jnp.int32, (16, MODEL), 0), 1.0, 0.0
    ).astype(BF16)
    key_inverse = lax.rsqrt(dot_nt(picks, upper) + dot_nt(picks, lower) + EPSILON)

    first = lax.broadcasted_iota(jnp.int32, (1, MODEL), 1) < HEAD

    def head_sums(array):
        low = jnp.sum(jnp.where(first, array, 0.0), axis=1, keepdims=True)
        high = jnp.sum(jnp.where(first, 0.0, array), axis=1, keepdims=True)
        return low, high

    for head in range(2):
        own_lanes = first if head == 0 else ~first
        raw[head] = dot_nt(jnp.where(own_lanes, queries[...], 0.0).astype(BF16), keys[...])
        dots[head] = dot_nt(jnp.where(own_lanes, d_attn[...], 0.0).astype(BF16), values[...])

    key_inv = [key_inverse[head : head + 1, :] for head in range(2)]
    wide = jnp.concatenate([scales[...]] * (KEYS // MODEL), axis=1)
    key_reach = [key_inv[head] * wide[head : head + 1, :] for head in range(2)]
    scale_lanes = jnp.where(first, scales[0:1, :], scales[1:2, :])
    scale_sums = [jnp.zeros((BLOCK, 1), F32), jnp.zeros((BLOCK, 1), F32)]
    for start in range(0, QUERIES, BLOCK):
        rows = slice(start, start + BLOCK)
        width = NEAR if start < OWN else KEYS
        query_wide = queries[rows, :].astype(F32)
        norms = head_sums(query_wide * query_wide)
        for head in range(2):
            inverse = lax.rsqrt(norms[head] + EPSILON)
            score = raw[head, rows, :width] * (inverse * LOG2E) * key_reach[head][:, :width]
            expo = jnp.exp2(score + bias[rows, :width])
            gain = dots[head, rows, :width]
            share = 1.0 / (jnp.sum(expo, axis=1, keepdims=True) + 1e-30)
            center = jnp.sum(expo * gain, axis=1, keepdims=True) * share
            if start < OWN:
                weight = expo[:, :NEAR] * share
                slope = weight * (gain[:, :NEAR] - center)
                pull = slope * key_inv[head][:, :NEAR]
                scale_sums[head] += inverse * jnp.sum(
                    pull * raw[head, rows, :NEAR], axis=1, keepdims=True
                )
                mix_own[head, rows, :] = weight.astype(BF16)
                slope_own[head, rows, :] = pull.astype(BF16)
                weight = weight[:, :OWN]
                slope = slope[:, :OWN]
            else:
                weight = expo[:, :OWN] * share
                slope = weight * (gain[:, :OWN] - center)
            mix_key[head, rows, :] = weight.astype(BF16)
            slope_key[head, rows, :] = (slope * inverse).astype(BF16)

    def both(dot, left, right):
        return jnp.where(first, dot(left[0], right), dot(left[1], right))

    attn_out = both(dot_nn, mix_own, values[0:NEAR, :]).astype(BF16)
    dq_unit = scale_lanes * both(dot_nn, slope_own, keys[0:NEAR, :])
    dk_unit = scale_lanes * both(dot_tn, slope_key, queries[...])
    dv = both(dot_tn, mix_key, d_attn[...])

    def unit_backward(vector, grad_unit):
        low, high = head_sums(vector * vector)
        inverse = jnp.where(first, lax.rsqrt(low + EPSILON), lax.rsqrt(high + EPSILON))
        unit = vector * inverse
        low, high = head_sums(unit * grad_unit)
        return (grad_unit - unit * jnp.where(first, low, high)) * inverse

    dq = unit_backward(queries[0:OWN, :].astype(F32), dq_unit).astype(BF16)
    dk = unit_backward(keys[0:OWN, :].astype(F32), dk_unit).astype(BF16)
    dv = dv.astype(BF16)
    grad_feat[...] = (
        dot_nt(dq, w_query)
        + dot_nt(dk, w_key)
        + dot_nt(dv, w_value)
    ).astype(BF16)
    norm = 1.0 / 256.0
    for part, grad in enumerate((dq, dk, dv)):
        grad_w[part * MODEL : (part + 1) * MODEL, :] = (
            dot_tn(tile[0:OWN, :], grad) * norm
        ).astype(BF16)
    grad_w[3 * MODEL :, :] = (dot_tn(attn_out, tile[OWN:, :]) * norm).astype(BF16)

    lane = lax.broadcasted_iota(jnp.int32, (8, MODEL), 1)
    part = lax.broadcasted_iota(jnp.int32, (8, MODEL), 0)
    terms = [jnp.sum(total, axis=0, keepdims=True) * norm for total in scale_sums]
    rest = jnp.where(part == 0, terms[0], terms[1])
    held = jnp.zeros((8, MODEL), F32)
    for which in range(3):
        piece = rest.astype(BF16).astype(F32)
        held = jnp.where(lane == which, piece, held)
        rest = rest - piece
    grad_scale[...] = held.astype(BF16)


def result_kernel(whole, terms, feat_tile, grad_feat, grad_w_qkv, grad_w_out, grad_scale):
    grad_feat[...] = feat_tile[...]
    for part in range(3):
        rows = slice(part * MODEL, (part + 1) * MODEL)
        grad_w_qkv[:, rows] = whole[rows, :].astype(F32)
    grad_w_out[...] = whole[3 * MODEL :, :].astype(F32)
    for head in range(2):
        grad_scale[head] = jnp.sum(terms[head : head + 1, :])


def pairs(target):
    found = []
    for row in range(16):
        for col in range(32):
            to_row, to_col = target(row, col)
            if 0 <= to_row < 16 and 0 <= to_col < 32:
                found.append((row * 32 + col, to_row * 32 + to_col))
    return found


EVERY = ("row", "col")


def device(x, y, z, core):
    return ((z % 8) * 2 + core) * 32 + (x % 4) * 8 + (y % 4) * 2 + z // 8 % 2


FIRST_X, FIRST_Y, FIRST_Z = 2, 2, 9
PLANES = [
    [
        device(x + FIRST_X, y + FIRST_Y, z, core)
        for x in range(4)
        for y in range(4)
        for core in (1, 0)
    ]
    for z in range(16)
]
LINES = [
    [device(x, y, z + FIRST_Z, core) for z in range(16)]
    for x in range(4)
    for y in range(4)
    for core in range(2)
]
CHIP_MATE = pairs(lambda row, col: (row ^ 1, col))
FAR_MATE = pairs(lambda row, col: (row, col - 1 if row % 2 else col + 1))
NEXT_CHIP = pairs(lambda row, col: (row + 1 if row % 2 else row - 1, col))
SKIP_CHIP = pairs(lambda row, col: (row - 2 if row % 2 else row + 2, col))


def exchange(array, groups):
    return lax.all_to_all(array, EVERY, 0, 0, axis_index_groups=groups, tiled=True)


def to_all(array, groups):
    return exchange(jnp.broadcast_to(array[None], (len(groups[0]),) + array.shape), groups)


def on_device(features, cotangent, w_qkv, w_out, cos_scale):
    feat = features.reshape(OWN, MODEL)
    cot = cotangent.reshape(OWN, MODEL)
    smem = pl.BlockSpec(memory_space=pltpu.SMEM)

    edge = jax.ShapeDtypeStruct((SENT, MODEL), BF16)
    tile = jnp.concatenate([feat, cot])
    own_edge, mate_message = pl.pallas_call(
        edge_kernel,
        out_shape=(edge, jax.ShapeDtypeStruct((SENT + 144, MODEL), BF16)),
        in_specs=vmem(1),
        out_specs=vmem(2),
        compiler_params=pltpu.CompilerParams(vmem_limit_bytes=2 * 1024 * 1024),
        name="edges",
    )(tile)
    mate = lax.ppermute(mate_message, EVERY, CHIP_MATE)
    other_edge = mate[:SENT]
    far = lax.ppermute(jnp.concatenate([own_edge, other_edge]), EVERY, FAR_MATE)
    key_spots = np.zeros((2, 16, KEYS), np.float32)
    key_spots[:, :2] = TABLES
    key_spots = jnp.asarray(key_spots)
    scales = jnp.broadcast_to(cos_scale[None, :, None], (4, 2, MODEL)).reshape(8, MODEL)
    tile_copy, weights, bias = pl.pallas_call(
        prepare_kernel,
        out_shape=(
            jax.ShapeDtypeStruct((2 * OWN, MODEL), BF16),
            jax.ShapeDtypeStruct((4 * MODEL, MODEL), BF16),
            jax.ShapeDtypeStruct((QUERIES, KEYS), F32),
        ),
        in_specs=vmem(5),
        out_specs=vmem(3),
        compiler_params=pltpu.CompilerParams(vmem_limit_bytes=4 * 1024 * 1024),
        cost_estimate=pl.CostEstimate(
            flops=1000000, bytes_accessed=1 << 20, transcendentals=0
        ),
        name="prepare",
    )(tile, mate, w_qkv, w_out, key_spots)
    next_chip = lax.ppermute(tile_copy, EVERY, NEXT_CHIP)

    far_mate = lax.ppermute(far, EVERY, CHIP_MATE)
    far_next = lax.ppermute(far, EVERY, NEXT_CHIP)
    far_skip = lax.ppermute(far, EVERY, SKIP_CHIP)
    grad_feat, grad_w, scale_tile = pl.pallas_call(
        attention_kernel,
        out_shape=(
            jax.ShapeDtypeStruct((OWN, MODEL), BF16),
            jax.ShapeDtypeStruct((4 * MODEL, MODEL), BF16),
            jax.ShapeDtypeStruct((8, MODEL), BF16),
        ),
        in_specs=vmem(10),
        out_specs=vmem(3),
        scratch_shapes=[
            pltpu.VMEM((KEYS, MODEL), BF16),
            pltpu.VMEM((QUERIES, MODEL), BF16),
            pltpu.VMEM((KEYS, MODEL), BF16),
            pltpu.VMEM((KEYS, MODEL), BF16),
            pltpu.VMEM((QUERIES, MODEL), BF16),
            pltpu.VMEM((QUERIES, MODEL), BF16),
            pltpu.VMEM((2, QUERIES, KEYS), F32),
            pltpu.VMEM((2, QUERIES, KEYS), F32),
            pltpu.VMEM((2, OWN, NEAR), BF16),
            pltpu.VMEM((2, QUERIES, OWN), BF16),
            pltpu.VMEM((2, OWN, NEAR), BF16),
            pltpu.VMEM((2, QUERIES, OWN), BF16),
        ],
        compiler_params=pltpu.CompilerParams(vmem_limit_bytes=16 * 1024 * 1024),
        name="window_attention",
    )(
        scales,
        tile,
        weights,
        mate,
        next_chip,
        far,
        far_skip,
        far_next,
        far_mate,
        bias,
    )

    scale_rows = jnp.broadcast_to(scale_tile[None, None, :2], (SHARES, 1, 2, MODEL))
    shares = jnp.concatenate([grad_w.reshape(SHARES, 8, 2, MODEL), scale_rows], axis=1)
    lane = lax.broadcasted_iota(jnp.int32, (2, MODEL), 1)
    shares, lane = lax.optimization_barrier((shares, lane))
    share = jnp.sum(exchange(shares, PLANES).astype(F32), axis=0)
    term = jnp.sum(jnp.where(lane < 3, share[8], 0.0), axis=1, keepdims=True)
    top = lax.reduce_precision(term, 8, 7)
    middle = lax.reduce_precision(term - top, 8, 7)
    parts = jnp.where(lane == 0, top, jnp.where(lane == 1, middle, term - top - middle))
    parts = jnp.where(lane < 3, parts, 0.0)
    share = jnp.concatenate([share[:8], parts[None]], axis=0).astype(BF16)
    share = jnp.sum(to_all(share, LINES).astype(F32), axis=0)
    share, terms = lax.optimization_barrier((share[:8].astype(BF16).reshape(16, MODEL), share[8]))
    whole = to_all(share, PLANES).reshape(4 * MODEL, MODEL)
    grad_feat, grad_w_qkv, grad_w_out, grad_scale = pl.pallas_call(
        result_kernel,
        out_shape=(
            jax.ShapeDtypeStruct((OWN, MODEL), BF16),
            jax.ShapeDtypeStruct((MODEL, 3 * MODEL), F32),
            jax.ShapeDtypeStruct((MODEL, MODEL), F32),
            jax.ShapeDtypeStruct((2,), F32),
        ),
        in_specs=vmem(3),
        out_specs=vmem(3) + [smem],
        compiler_params=pltpu.CompilerParams(vmem_limit_bytes=2 * 1024 * 1024),
        name="results",
    )(whole, terms, grad_feat)
    return (grad_feat.reshape(ROWS, COLS, MODEL), grad_w_qkv, grad_w_out, grad_scale)


def solution(mesh):
    tokens = P("row", "col", None)
    return jax.shard_map(
        on_device,
        mesh=mesh,
        in_specs=(tokens, tokens, P(), P(), P()),
        out_specs=(tokens, P(), P(), P()),
        check_vma=False,
    )
```

```python
import functools

import jax
import jax.numpy as jnp
import numpy as np
from jax import lax
from jax.experimental import pallas as pl
from jax.experimental.pallas import tpu as pltpu
from jax.sharding import PartitionSpec as P

RADIUS = 3
EPSILON = 1e-06
MODEL = 128
HEAD = 64
ROWS, COLS = 8, 16
OWN = ROWS * COLS
QUERIES = 368
KEYS = 640
NEAR = 384
BLOCK = 16
EDGE = 24
SENT = 80
SHARES = 32
LOG2E = 1.4426950408889634
FAR_AWAY = 1e4

F32 = jnp.float32
BF16 = jnp.bfloat16


def side_columns(left, inner):
    if left:
        return -3 if inner else -6
    return 16 if inner else 19


def token_table(core):
    def tile(holder, start, count, lift):
        token = start + np.arange(count)
        return np.stack([8 * holder + token // 16 + lift, token % 16])

    def edge(holder, left, inner, lift):
        token = np.arange(EDGE)
        row = 8 * holder + token // 3 + lift
        return np.stack([row, token % 3 + side_columns(left, inner)])

    other = 1 - core
    lift = -16 if core == 0 else 16
    left = core == 0
    pieces = [
        tile(core, 0, 128, 0),
        tile(other, 80 * core, 48, 0),
        edge(core, left, True, 0),
        edge(other, left, True, 0),
        edge(other, not left, True, 0),
        edge(core, not left, True, 0),
        tile(other, 80 * other, 48, lift),
        edge(other, not left, True, lift),
        edge(other, left, True, lift),
        tile(other, 48 - 16 * core, 48, 0),
        edge(core, left, False, 0),
        edge(other, left, False, 0),
        edge(other, not left, False, 0),
        edge(core, not left, False, 0),
        tile(other, 48 - 16 * other, 48, lift),
        edge(other, not left, False, lift),
        edge(other, left, False, lift),
        np.full((2, 32), FAR_AWAY),
    ]
    return np.concatenate(pieces, axis=1).astype(np.float32)


TABLES = np.stack([token_table(0), token_table(1)])


def vmem(count):
    return [pl.BlockSpec(memory_space=pltpu.VMEM)] * count


def dot_nt(left, right):
    return lax.dot_general(
        left, right, (((1,), (1,)), ((), ())), preferred_element_type=F32
    )


def dot_tn(left, right):
    return lax.dot_general(
        left, right, (((0,), (0,)), ((), ())), preferred_element_type=F32
    )


def dot_nn(left, right):
    return jnp.dot(left, right, preferred_element_type=F32)


def edge_kernel(tile, own_edge, mate_message):
    core, _, _ = place_here()
    spot = lax.broadcasted_iota(jnp.int32, (SENT, 128), 0)
    token = lax.broadcasted_iota(jnp.int32, (SENT, 128), 1)
    kind = jnp.where(spot >= EDGE, 1, 0) + jnp.where(spot >= 2 * EDGE, 1, 0)
    index = spot - EDGE * kind
    row = (index * 43) >> 7
    step = index - 3 * row
    outer = kind == 1
    right = row * 16 + step + jnp.where(outer, 10, 13)
    left = row * 16 + step + jnp.where(outer, 3, 0)
    used = spot < 3 * EDGE
    from_cot = kind == 2
    for ref, wanted in (
        (own_edge, jnp.where(core == 0, right, left)),
        (mate_message, jnp.where(core == 0, left, right)),
    ):
        hit = (wanted == token) & used
        of_feat = jnp.where(hit & ~from_cot, 1.0, 0.0).astype(BF16)
        of_cot = jnp.where(hit & from_cot, 1.0, 0.0).astype(BF16)
        ref[0:SENT, :] = (
            dot_nn(of_feat, tile[0:OWN, :]) + dot_nn(of_cot, tile[OWN:, :])
        ).astype(BF16)
    half = 1 - core
    mate_message[SENT : SENT + 48, :] = rows_at(tile, 80 * half, 48)
    mate_message[SENT + 48 : SENT + 96, :] = rows_at(tile, 48 - 16 * half, 48)
    mate_message[SENT + 96 : SENT + 144, :] = rows_at(tile, OWN + 80 * half, 48)


def place_here():
    row, col = lax.axis_index("row"), lax.axis_index("col")
    return row & 1, (row >> 1) * 16, col * 16


def rows_at(ref, start, count):
    return ref[pl.ds(pl.multiple_of(start, 16), count), :]


def prepare_kernel(tile, _, w_qkv, w_out, key_spots, tile_copy, weights, bias):
    tile_copy[...] = tile[...]
    for part in range(3):
        columns = slice(part * MODEL, (part + 1) * MODEL)
        weights[columns, :] = w_qkv[:, columns]
    weights[3 * MODEL :, :] = w_out[...]

    core, first_row, first_col = place_here()
    spots = jnp.where(core == 0, key_spots[0], key_spots[1])
    key_rows, key_cols = spots[0:1, :], spots[1:2, :]
    turn = lax.broadcasted_iota(jnp.int32, (16, MODEL), 0)
    turn = jnp.where(turn == lax.broadcasted_iota(jnp.int32, (16, MODEL), 1), 1.0, 0.0)
    query_spots = dot_tn(spots[:, :NEAR].astype(BF16), turn.astype(BF16))
    all_rows = key_rows + first_row.astype(F32)
    all_cols = key_cols + first_col.astype(F32)
    inside = (all_rows >= 0) & (all_rows < 128) & (all_cols >= 0) & (all_cols < 512)
    key_rows = jnp.where(inside, key_rows, FAR_AWAY)
    for start in range(0, QUERIES, BLOCK):
        here = query_spots[start : start + BLOCK, :]
        apart = jnp.maximum(
            jnp.abs(here[:, 0:1] - key_rows), jnp.abs(here[:, 1:2] - key_cols)
        )
        bias[start : start + BLOCK, :] = jnp.where(apart <= RADIUS, 0.0, -1e30)


def attention_kernel(
    scales,
    tile,
    weights,
    mate,
    next_chip,
    far,
    far_skip,
    far_next,
    far_mate,
    bias,
    grad_feat,
    grad_w,
    grad_scale,
    tokens,
    cots,
    keys,
    values,
    queries,
    d_attn,
    raw,
    dots,
    mix_own,
    mix_key,
    slope_own,
    slope_key,
):
    core, _, _ = place_here()
    other = 1 - core
    w_query, w_key, w_value, w_out = (
        weights[start : start + MODEL, :] for start in range(0, 4 * MODEL, MODEL)
    )
    far_wide = far[...].astype(F32)
    mate_wide = far_mate[...].astype(F32)
    next_wide = far_next[0:SENT, :].astype(F32)
    skip_wide = far_skip[SENT:, :].astype(F32)
    edges = (
        far_wide[:SENT],
        far_wide[SENT:],
        mate_wide[:SENT],
        mate_wide[SENT:],
        next_wide,
        skip_wide,
    )

    def strip(kind, chosen):
        pieces = [edge[kind * EDGE : (kind + 1) * EDGE] for edge in chosen]
        return jnp.concatenate(pieces, axis=0).astype(BF16)

    tokens[0:128, :] = tile[0:OWN, :]
    tokens[128:176, :] = mate[SENT : SENT + 48, :]
    tokens[176:272, :] = strip(0, edges[:4])
    tokens[272:320, :] = rows_at(next_chip, 80 * other, 48)
    tokens[320:368, :] = strip(0, edges[4:])
    tokens[368:416, :] = mate[SENT + 48 : SENT + 96, :]
    tokens[416:512, :] = strip(1, edges[:4])
    tokens[512:560, :] = rows_at(next_chip, 48 - 16 * other, 48)
    tokens[560:608, :] = strip(1, edges[4:])
    tokens[608:640, :] = jnp.zeros((32, MODEL), BF16)
    cots[0:128, :] = tile[OWN:, :]
    cots[128:176, :] = mate[SENT + 96 : SENT + 144, :]
    cots[176:272, :] = strip(2, edges[:4])
    cots[272:320, :] = rows_at(next_chip, OWN + 80 * other, 48)
    cots[320:368, :] = strip(2, edges[4:])

    keys[...] = dot_nn(tokens[...], w_key).astype(BF16)
    values[...] = dot_nn(tokens[...], w_value).astype(BF16)
    queries[...] = dot_nn(tokens[0:QUERIES, :], w_query).astype(BF16)
    d_attn[...] = dot_nt(cots[...], w_out).astype(BF16)

    key_wide = keys[...].astype(F32)
    square = key_wide * key_wide
    upper = square.astype(BF16)
    lower = (square - upper.astype(F32)).astype(BF16)
    head_of = lax.broadcasted_iota(jnp.int32, (16, MODEL), 1) // HEAD
    picks = jnp.where(
        head_of == lax.broadcasted_iota(jnp.int32, (16, MODEL), 0), 1.0, 0.0
    ).astype(BF16)
    key_inverse = lax.rsqrt(dot_nt(picks, upper) + dot_nt(picks, lower) + EPSILON)

    first = lax.broadcasted_iota(jnp.int32, (1, MODEL), 1) < HEAD

    def head_sums(array):
        low = jnp.sum(jnp.where(first, array, 0.0), axis=1, keepdims=True)
        high = jnp.sum(jnp.where(first, 0.0, array), axis=1, keepdims=True)
        return low, high

    for head in range(2):
        own_lanes = first if head == 0 else ~first
        raw[head] = dot_nt(jnp.where(own_lanes, queries[...], 0.0).astype(BF16), keys[...])
        dots[head] = dot_nt(jnp.where(own_lanes, d_attn[...], 0.0).astype(BF16), values[...])

    key_inv = [key_inverse[head : head + 1, :] for head in range(2)]
    wide = jnp.concatenate([scales[...]] * (KEYS // MODEL), axis=1)
    key_reach = [key_inv[head] * wide[head : head + 1, :] for head in range(2)]
    scale_lanes = jnp.where(first, scales[0:1, :], scales[1:2, :])
    scale_sums = [jnp.zeros((BLOCK, 1), F32), jnp.zeros((BLOCK, 1), F32)]
    for start in range(0, QUERIES, BLOCK):
        rows = slice(start, start + BLOCK)
        width = NEAR if start < OWN else KEYS
        query_wide = queries[rows, :].astype(F32)
        norms = head_sums(query_wide * query_wide)
        for head in range(2):
            inverse = lax.rsqrt(norms[head] + EPSILON)
            score = raw[head, rows, :width] * (inverse * LOG2E) * key_reach[head][:, :width]
            expo = jnp.exp2(score + bias[rows, :width])
            gain = dots[head, rows, :width]
            share = 1.0 / (jnp.sum(expo, axis=1, keepdims=True) + 1e-30)
            center = jnp.sum(expo * gain, axis=1, keepdims=True) * share
            if start < OWN:
                weight = expo[:, :NEAR] * share
                slope = weight * (gain[:, :NEAR] - center)
                pull = slope * key_inv[head][:, :NEAR]
                scale_sums[head] += inverse * jnp.sum(
                    pull * raw[head, rows, :NEAR], axis=1, keepdims=True
                )
                mix_own[head, rows, :] = weight.astype(BF16)
                slope_own[head, rows, :] = pull.astype(BF16)
                weight = weight[:, :OWN]
                slope = slope[:, :OWN]
            else:
                weight = expo[:, :OWN] * share
                slope = weight * (gain[:, :OWN] - center)
            mix_key[head, rows, :] = weight.astype(BF16)
            slope_key[head, rows, :] = (slope * inverse).astype(BF16)

    def both(dot, left, right):
        return jnp.where(first, dot(left[0], right), dot(left[1], right))

    attn_out = both(dot_nn, mix_own, values[0:NEAR, :]).astype(BF16)
    dq_unit = scale_lanes * both(dot_nn, slope_own, keys[0:NEAR, :])
    dk_unit = scale_lanes * both(dot_tn, slope_key, queries[...])
    dv = both(dot_tn, mix_key, d_attn[...])

    def unit_backward(vector, grad_unit):
        low, high = head_sums(vector * vector)
        inverse = jnp.where(first, lax.rsqrt(low + EPSILON), lax.rsqrt(high + EPSILON))
        unit = vector * inverse
        low, high = head_sums(unit * grad_unit)
        return (grad_unit - unit * jnp.where(first, low, high)) * inverse

    dq = unit_backward(queries[0:OWN, :].astype(F32), dq_unit).astype(BF16)
    dk = unit_backward(keys[0:OWN, :].astype(F32), dk_unit).astype(BF16)
    dv = dv.astype(BF16)
    grad_feat[...] = (
        dot_nt(dq, w_query)
        + dot_nt(dk, w_key)
        + dot_nt(dv, w_value)
    ).astype(BF16)
    norm = 1.0 / 256.0
    for part, grad in enumerate((dq, dk, dv)):
        grad_w[part * MODEL : (part + 1) * MODEL, :] = (
            dot_tn(tile[0:OWN, :], grad) * norm
        ).astype(BF16)
    grad_w[3 * MODEL :, :] = (dot_tn(attn_out, tile[OWN:, :]) * norm).astype(BF16)

    lane = lax.broadcasted_iota(jnp.int32, (8, MODEL), 1)
    part = lax.broadcasted_iota(jnp.int32, (8, MODEL), 0)
    terms = [jnp.sum(total, axis=0, keepdims=True) * norm for total in scale_sums]
    rest = jnp.where(part == 0, terms[0], terms[1])
    held = jnp.zeros((8, MODEL), F32)
    for which in range(3):
        piece = rest.astype(BF16).astype(F32)
        held = jnp.where(lane == which, piece, held)
        rest = rest - piece
    grad_scale[...] = held.astype(BF16)


def result_kernel(whole, terms, feat_tile, grad_feat, grad_w_qkv, grad_w_out, grad_scale):
    grad_feat[...] = feat_tile[...]
    for part in range(3):
        rows = slice(part * MODEL, (part + 1) * MODEL)
        grad_w_qkv[:, rows] = whole[rows, :].astype(F32)
    grad_w_out[...] = whole[3 * MODEL :, :].astype(F32)
    for head in range(2):
        grad_scale[head] = jnp.sum(terms[head : head + 1, :])


def pairs(target):
    found = []
    for row in range(16):
        for col in range(32):
            to_row, to_col = target(row, col)
            if 0 <= to_row < 16 and 0 <= to_col < 32:
                found.append((row * 32 + col, to_row * 32 + to_col))
    return found


EVERY = ("row", "col")


def device(x, y, z, core):
    return ((z % 8) * 2 + core) * 32 + (x % 4) * 8 + (y % 4) * 2 + z // 8 % 2


FIRST_X, FIRST_Y, FIRST_Z = 2, 2, 9
def apart(place):
    return min(place[0], 4 - place[0]) + min(place[1], 4 - place[1])


PLACES = sorted(
    ((x, y, core) for x in range(4) for y in range(4) for core in (1, 0)),
    key=lambda place: (place != (0, 0, 1), -apart(place)),
)
PLANES = [
    [device(x + FIRST_X, y + FIRST_Y, z, core) for x, y, core in PLACES] for z in range(16)
]
LINES = [
    [device(x, y, z + FIRST_Z, core) for z in range(16)]
    for x in range(4)
    for y in range(4)
    for core in range(2)
]
CHIP_MATE = pairs(lambda row, col: (row ^ 1, col))
FAR_MATE = pairs(lambda row, col: (row, col - 1 if row % 2 else col + 1))
NEXT_CHIP = pairs(lambda row, col: (row + 1 if row % 2 else row - 1, col))
SKIP_CHIP = pairs(lambda row, col: (row - 2 if row % 2 else row + 2, col))


def exchange(array, groups):
    return lax.all_to_all(array, EVERY, 0, 0, axis_index_groups=groups, tiled=True)


def to_all(array, groups):
    return exchange(jnp.broadcast_to(array[None], (len(groups[0]),) + array.shape), groups)


def on_device(features, cotangent, w_qkv, w_out, cos_scale):
    feat = features.reshape(OWN, MODEL)
    cot = cotangent.reshape(OWN, MODEL)
    smem = pl.BlockSpec(memory_space=pltpu.SMEM)

    edge = jax.ShapeDtypeStruct((SENT, MODEL), BF16)
    tile = jnp.concatenate([feat, cot])
    own_edge, mate_message = pl.pallas_call(
        edge_kernel,
        out_shape=(edge, jax.ShapeDtypeStruct((SENT + 144, MODEL), BF16)),
        in_specs=vmem(1),
        out_specs=vmem(2),
        compiler_params=pltpu.CompilerParams(vmem_limit_bytes=2 * 1024 * 1024),
        name="edges",
    )(tile)
    mate = lax.ppermute(mate_message, EVERY, CHIP_MATE)
    other_edge = mate[:SENT]
    far = lax.ppermute(jnp.concatenate([own_edge, other_edge]), EVERY, FAR_MATE)
    key_spots = np.zeros((2, 16, KEYS), np.float32)
    key_spots[:, :2] = TABLES
    key_spots = jnp.asarray(key_spots)
    scales = jnp.broadcast_to(cos_scale[None, :, None], (4, 2, MODEL)).reshape(8, MODEL)
    tile_copy, weights, bias = pl.pallas_call(
        prepare_kernel,
        out_shape=(
            jax.ShapeDtypeStruct((2 * OWN, MODEL), BF16),
            jax.ShapeDtypeStruct((4 * MODEL, MODEL), BF16),
            jax.ShapeDtypeStruct((QUERIES, KEYS), F32),
        ),
        in_specs=vmem(5),
        out_specs=vmem(3),
        compiler_params=pltpu.CompilerParams(vmem_limit_bytes=4 * 1024 * 1024),
        cost_estimate=pl.CostEstimate(
            flops=1000000, bytes_accessed=1 << 20, transcendentals=0
        ),
        name="prepare",
    )(tile, mate, w_qkv, w_out, key_spots)
    next_chip = lax.ppermute(tile_copy, EVERY, NEXT_CHIP)

    far_mate = lax.ppermute(far, EVERY, CHIP_MATE)
    far_next = lax.ppermute(far, EVERY, NEXT_CHIP)
    far_skip = lax.ppermute(far, EVERY, SKIP_CHIP)
    grad_feat, grad_w, scale_tile = pl.pallas_call(
        attention_kernel,
        out_shape=(
            jax.ShapeDtypeStruct((OWN, MODEL), BF16),
            jax.ShapeDtypeStruct((4 * MODEL, MODEL), BF16),
            jax.ShapeDtypeStruct((8, MODEL), BF16),
        ),
        in_specs=vmem(10),
        out_specs=vmem(3),
        scratch_shapes=[
            pltpu.VMEM((KEYS, MODEL), BF16),
            pltpu.VMEM((QUERIES, MODEL), BF16),
            pltpu.VMEM((KEYS, MODEL), BF16),
            pltpu.VMEM((KEYS, MODEL), BF16),
            pltpu.VMEM((QUERIES, MODEL), BF16),
            pltpu.VMEM((QUERIES, MODEL), BF16),
            pltpu.VMEM((2, QUERIES, KEYS), F32),
            pltpu.VMEM((2, QUERIES, KEYS), F32),
            pltpu.VMEM((2, OWN, NEAR), BF16),
            pltpu.VMEM((2, QUERIES, OWN), BF16),
            pltpu.VMEM((2, OWN, NEAR), BF16),
            pltpu.VMEM((2, QUERIES, OWN), BF16),
        ],
        compiler_params=pltpu.CompilerParams(vmem_limit_bytes=16 * 1024 * 1024),
        name="window_attention",
    )(
        scales,
        tile,
        weights,
        mate,
        next_chip,
        far,
        far_skip,
        far_next,
        far_mate,
        bias,
    )

    scale_rows = jnp.broadcast_to(scale_tile[None, None, :2], (SHARES, 1, 2, MODEL))
    shares = jnp.concatenate([grad_w.reshape(SHARES, 8, 2, MODEL), scale_rows], axis=1)
    lane = lax.broadcasted_iota(jnp.int32, (2, MODEL), 1)
    shares, lane = lax.optimization_barrier((shares, lane))
    share = jnp.sum(exchange(shares, PLANES).astype(F32), axis=0)
    term = jnp.sum(jnp.where(lane < 3, share[8], 0.0), axis=1, keepdims=True)
    top = lax.reduce_precision(term, 8, 7)
    middle = lax.reduce_precision(term - top, 8, 7)
    parts = jnp.where(lane == 0, top, jnp.where(lane == 1, middle, term - top - middle))
    parts = jnp.where(lane < 3, parts, 0.0)
    share = jnp.concatenate([share[:8], parts[None]], axis=0).astype(BF16)
    share = jnp.sum(to_all(share, LINES).astype(F32), axis=0)
    share, terms = lax.optimization_barrier((share[:8].astype(BF16).reshape(16, MODEL), share[8]))
    whole = to_all(share, PLANES).reshape(4 * MODEL, MODEL)
    grad_feat, grad_w_qkv, grad_w_out, grad_scale = pl.pallas_call(
        result_kernel,
        out_shape=(
            jax.ShapeDtypeStruct((OWN, MODEL), BF16),
            jax.ShapeDtypeStruct((MODEL, 3 * MODEL), F32),
            jax.ShapeDtypeStruct((MODEL, MODEL), F32),
            jax.ShapeDtypeStruct((2,), F32),
        ),
        in_specs=vmem(3),
        out_specs=vmem(3) + [smem],
        compiler_params=pltpu.CompilerParams(vmem_limit_bytes=2 * 1024 * 1024),
        name="results",
    )(whole, terms, grad_feat)
    return (grad_feat.reshape(ROWS, COLS, MODEL), grad_w_qkv, grad_w_out, grad_scale)


def solution(mesh):
    tokens = P("row", "col", None)
    return jax.shard_map(
        on_device,
        mesh=mesh,
        in_specs=(tokens, tokens, P(), P(), P()),
        out_specs=(tokens, P(), P(), P()),
        check_vma=False,
    )
```

```python
import functools

import jax
import jax.numpy as jnp
import numpy as np
from jax import lax
from jax.experimental import pallas as pl
from jax.experimental.pallas import tpu as pltpu
from jax.sharding import PartitionSpec as P

RADIUS = 3
EPSILON = 1e-06
MODEL = 128
HEAD = 64
ROWS, COLS = 8, 16
OWN = ROWS * COLS
QUERIES = 368
KEYS = 640
NEAR = 384
BLOCK = 16
EDGE = 24
SENT = 80
SHARES = 32
LOG2E = 1.4426950408889634
FAR_AWAY = 1e4

F32 = jnp.float32
BF16 = jnp.bfloat16


def side_columns(left, inner):
    if left:
        return -3 if inner else -6
    return 16 if inner else 19


def token_table(core):
    def tile(holder, start, count, lift):
        token = start + np.arange(count)
        return np.stack([8 * holder + token // 16 + lift, token % 16])

    def edge(holder, left, inner, lift):
        token = np.arange(EDGE)
        row = 8 * holder + token // 3 + lift
        return np.stack([row, token % 3 + side_columns(left, inner)])

    other = 1 - core
    lift = -16 if core == 0 else 16
    left = core == 0
    pieces = [
        tile(core, 0, 128, 0),
        tile(other, 80 * core, 48, 0),
        edge(core, left, True, 0),
        edge(other, left, True, 0),
        edge(other, not left, True, 0),
        edge(core, not left, True, 0),
        tile(other, 80 * other, 48, lift),
        edge(other, not left, True, lift),
        edge(other, left, True, lift),
        tile(other, 48 - 16 * core, 48, 0),
        edge(core, left, False, 0),
        edge(other, left, False, 0),
        edge(other, not left, False, 0),
        edge(core, not left, False, 0),
        tile(other, 48 - 16 * other, 48, lift),
        edge(other, not left, False, lift),
        edge(other, left, False, lift),
        np.full((2, 32), FAR_AWAY),
    ]
    return np.concatenate(pieces, axis=1).astype(np.float32)


TABLES = np.stack([token_table(0), token_table(1)])


def vmem(count):
    return [pl.BlockSpec(memory_space=pltpu.VMEM)] * count


def dot_nt(left, right):
    return lax.dot_general(
        left, right, (((1,), (1,)), ((), ())), preferred_element_type=F32
    )


def dot_tn(left, right):
    return lax.dot_general(
        left, right, (((0,), (0,)), ((), ())), preferred_element_type=F32
    )


def dot_nn(left, right):
    return jnp.dot(left, right, preferred_element_type=F32)


def edge_kernel(tile, own_edge, mate_message):
    core, _, _ = place_here()
    spot = lax.broadcasted_iota(jnp.int32, (SENT, 128), 0)
    token = lax.broadcasted_iota(jnp.int32, (SENT, 128), 1)
    kind = jnp.where(spot >= EDGE, 1, 0) + jnp.where(spot >= 2 * EDGE, 1, 0)
    index = spot - EDGE * kind
    row = (index * 43) >> 7
    step = index - 3 * row
    outer = kind == 1
    right = row * 16 + step + jnp.where(outer, 10, 13)
    left = row * 16 + step + jnp.where(outer, 3, 0)
    used = spot < 3 * EDGE
    from_cot = kind == 2
    for ref, wanted in (
        (own_edge, jnp.where(core == 0, right, left)),
        (mate_message, jnp.where(core == 0, left, right)),
    ):
        hit = (wanted == token) & used
        of_feat = jnp.where(hit & ~from_cot, 1.0, 0.0).astype(BF16)
        of_cot = jnp.where(hit & from_cot, 1.0, 0.0).astype(BF16)
        ref[0:SENT, :] = (
            dot_nn(of_feat, tile[0:OWN, :]) + dot_nn(of_cot, tile[OWN:, :])
        ).astype(BF16)
    half = 1 - core
    mate_message[SENT : SENT + 48, :] = rows_at(tile, 80 * half, 48)
    mate_message[SENT + 48 : SENT + 96, :] = rows_at(tile, 48 - 16 * half, 48)
    mate_message[SENT + 96 : SENT + 144, :] = rows_at(tile, OWN + 80 * half, 48)


def place_here():
    row, col = lax.axis_index("row"), lax.axis_index("col")
    return row & 1, (row >> 1) * 16, col * 16


def rows_at(ref, start, count):
    return ref[pl.ds(pl.multiple_of(start, 16), count), :]


def prepare_kernel(tile, _, w_qkv, w_out, key_spots, tile_copy, weights, bias):
    tile_copy[...] = tile[...]
    for part in range(3):
        columns = slice(part * MODEL, (part + 1) * MODEL)
        weights[columns, :] = w_qkv[:, columns]
    weights[3 * MODEL :, :] = w_out[...]

    core, first_row, first_col = place_here()
    spots = jnp.where(core == 0, key_spots[0], key_spots[1])
    key_rows, key_cols = spots[0:1, :], spots[1:2, :]
    turn = lax.broadcasted_iota(jnp.int32, (16, MODEL), 0)
    turn = jnp.where(turn == lax.broadcasted_iota(jnp.int32, (16, MODEL), 1), 1.0, 0.0)
    query_spots = dot_tn(spots[:, :NEAR].astype(BF16), turn.astype(BF16))
    all_rows = key_rows + first_row.astype(F32)
    all_cols = key_cols + first_col.astype(F32)
    inside = (all_rows >= 0) & (all_rows < 128) & (all_cols >= 0) & (all_cols < 512)
    key_rows = jnp.where(inside, key_rows, FAR_AWAY)
    for start in range(0, QUERIES, BLOCK):
        here = query_spots[start : start + BLOCK, :]
        apart = jnp.maximum(
            jnp.abs(here[:, 0:1] - key_rows), jnp.abs(here[:, 1:2] - key_cols)
        )
        bias[start : start + BLOCK, :] = jnp.where(apart <= RADIUS, 0.0, -1e30)


def attention_kernel(
    scales,
    tile,
    weights,
    mate,
    next_chip,
    far,
    far_skip,
    far_next,
    far_mate,
    bias,
    grad_feat,
    grad_w,
    grad_scale,
    tokens,
    cots,
    keys,
    values,
    queries,
    d_attn,
    raw,
    dots,
    mix_own,
    mix_key,
    slope_own,
    slope_key,
):
    core, _, _ = place_here()
    other = 1 - core
    w_query, w_key, w_value, w_out = (
        weights[start : start + MODEL, :] for start in range(0, 4 * MODEL, MODEL)
    )
    far_wide = far[...].astype(F32)
    mate_wide = far_mate[...].astype(F32)
    next_wide = far_next[0:SENT, :].astype(F32)
    skip_wide = far_skip[SENT:, :].astype(F32)
    edges = (
        far_wide[:SENT],
        far_wide[SENT:],
        mate_wide[:SENT],
        mate_wide[SENT:],
        next_wide,
        skip_wide,
    )

    def strip(kind, chosen):
        pieces = [edge[kind * EDGE : (kind + 1) * EDGE] for edge in chosen]
        return jnp.concatenate(pieces, axis=0).astype(BF16)

    tokens[0:128, :] = tile[0:OWN, :]
    tokens[128:176, :] = mate[SENT : SENT + 48, :]
    tokens[176:272, :] = strip(0, edges[:4])
    tokens[272:320, :] = rows_at(next_chip, 80 * other, 48)
    tokens[320:368, :] = strip(0, edges[4:])
    tokens[368:416, :] = mate[SENT + 48 : SENT + 96, :]
    tokens[416:512, :] = strip(1, edges[:4])
    tokens[512:560, :] = rows_at(next_chip, 48 - 16 * other, 48)
    tokens[560:608, :] = strip(1, edges[4:])
    tokens[608:640, :] = jnp.zeros((32, MODEL), BF16)
    cots[0:128, :] = tile[OWN:, :]
    cots[128:176, :] = mate[SENT + 96 : SENT + 144, :]
    cots[176:272, :] = strip(2, edges[:4])
    cots[272:320, :] = rows_at(next_chip, OWN + 80 * other, 48)
    cots[320:368, :] = strip(2, edges[4:])

    both_kinds = dot_nn(tokens[...], jnp.concatenate([w_key, w_value], axis=1)).astype(BF16)
    keys[...] = both_kinds[:, :MODEL]
    values[...] = both_kinds[:, MODEL:]
    queries[...] = dot_nn(tokens[0:QUERIES, :], w_query).astype(BF16)
    d_attn[...] = dot_nt(cots[...], w_out).astype(BF16)

    key_wide = keys[...].astype(F32)
    square = key_wide * key_wide
    upper = square.astype(BF16)
    lower = (square - upper.astype(F32)).astype(BF16)
    head_of = lax.broadcasted_iota(jnp.int32, (16, MODEL), 1) // HEAD
    picks = jnp.where(
        head_of == lax.broadcasted_iota(jnp.int32, (16, MODEL), 0), 1.0, 0.0
    ).astype(BF16)
    key_inverse = lax.rsqrt(dot_nt(picks, upper) + dot_nt(picks, lower) + EPSILON)

    first = lax.broadcasted_iota(jnp.int32, (1, MODEL), 1) < HEAD

    def head_sums(array):
        low = jnp.sum(jnp.where(first, array, 0.0), axis=1, keepdims=True)
        high = jnp.sum(jnp.where(first, 0.0, array), axis=1, keepdims=True)
        return low, high

    for head in range(2):
        own_lanes = first if head == 0 else ~first
        for rows, width in ((slice(0, OWN), NEAR), (slice(OWN, QUERIES), KEYS)):
            query = jnp.where(own_lanes, queries[rows, :], 0.0).astype(BF16)
            grad = jnp.where(own_lanes, d_attn[rows, :], 0.0).astype(BF16)
            raw[head, rows, :width] = dot_nt(query, keys[0:width, :])
            dots[head, rows, :width] = dot_nt(grad, values[0:width, :])

    key_inv = [key_inverse[head : head + 1, :] for head in range(2)]
    wide = jnp.concatenate([scales[...]] * (KEYS // MODEL), axis=1)
    key_reach = [key_inv[head] * wide[head : head + 1, :] for head in range(2)]
    scale_lanes = jnp.where(first, scales[0:1, :], scales[1:2, :])
    scale_sums = [jnp.zeros((BLOCK, 1), F32), jnp.zeros((BLOCK, 1), F32)]
    for start in range(0, QUERIES, BLOCK):
        rows = slice(start, start + BLOCK)
        width = NEAR if start < OWN else KEYS
        query_wide = queries[rows, :].astype(F32)
        norms = head_sums(query_wide * query_wide)
        for head in range(2):
            inverse = lax.rsqrt(norms[head] + EPSILON)
            score = raw[head, rows, :width] * (inverse * LOG2E) * key_reach[head][:, :width]
            expo = jnp.exp2(score + bias[rows, :width])
            gain = dots[head, rows, :width]
            share = 1.0 / (jnp.sum(expo, axis=1, keepdims=True) + 1e-30)
            center = jnp.sum(expo * gain, axis=1, keepdims=True) * share
            if start < OWN:
                weight = expo[:, :NEAR] * share
                slope = weight * (gain[:, :NEAR] - center)
                pull = slope * key_inv[head][:, :NEAR]
                scale_sums[head] += inverse * jnp.sum(
                    pull * raw[head, rows, :NEAR], axis=1, keepdims=True
                )
                mix_own[head, rows, :] = weight.astype(BF16)
                slope_own[head, rows, :] = pull.astype(BF16)
                weight = weight[:, :OWN]
                slope = slope[:, :OWN]
            else:
                weight = expo[:, :OWN] * share
                slope = weight * (gain[:, :OWN] - center)
            mix_key[head, rows, :] = weight.astype(BF16)
            slope_key[head, rows, :] = (slope * inverse).astype(BF16)

    def both(dot, left, right):
        return jnp.where(first, dot(left[0], right), dot(left[1], right))

    attn_out = both(dot_nn, mix_own, values[0:NEAR, :]).astype(BF16)
    dq_unit = scale_lanes * both(dot_nn, slope_own, keys[0:NEAR, :])
    dk_unit = scale_lanes * both(dot_tn, slope_key, queries[...])
    dv = both(dot_tn, mix_key, d_attn[...])

    def unit_backward(vector, grad_unit):
        low, high = head_sums(vector * vector)
        inverse = jnp.where(first, lax.rsqrt(low + EPSILON), lax.rsqrt(high + EPSILON))
        unit = vector * inverse
        low, high = head_sums(unit * grad_unit)
        return (grad_unit - unit * jnp.where(first, low, high)) * inverse

    dq = unit_backward(queries[0:OWN, :].astype(F32), dq_unit).astype(BF16)
    dk = unit_backward(keys[0:OWN, :].astype(F32), dk_unit).astype(BF16)
    dv = dv.astype(BF16)
    grad_feat[...] = (
        dot_nt(dq, w_query)
        + dot_nt(dk, w_key)
        + dot_nt(dv, w_value)
    ).astype(BF16)
    norm = 1.0 / 256.0
    for part, grad in enumerate((dq, dk, dv)):
        grad_w[part * MODEL : (part + 1) * MODEL, :] = (
            dot_tn(tile[0:OWN, :], grad) * norm
        ).astype(BF16)
    grad_w[3 * MODEL :, :] = (dot_tn(attn_out, tile[OWN:, :]) * norm).astype(BF16)

    lane = lax.broadcasted_iota(jnp.int32, (8, MODEL), 1)
    part = lax.broadcasted_iota(jnp.int32, (8, MODEL), 0)
    terms = [jnp.sum(total, axis=0, keepdims=True) * norm for total in scale_sums]
    rest = jnp.where(part == 0, terms[0], terms[1])
    held = jnp.zeros((8, MODEL), F32)
    for which in range(3):
        piece = rest.astype(BF16).astype(F32)
        held = jnp.where(lane == which, piece, held)
        rest = rest - piece
    grad_scale[...] = held.astype(BF16)


def result_kernel(whole, terms, feat_tile, grad_feat, grad_w_qkv, grad_w_out, grad_scale):
    grad_feat[...] = feat_tile[...]
    for part in range(3):
        rows = slice(part * MODEL, (part + 1) * MODEL)
        grad_w_qkv[:, rows] = whole[rows, :].astype(F32)
    grad_w_out[...] = whole[3 * MODEL :, :].astype(F32)
    for head in range(2):
        grad_scale[head] = jnp.sum(terms[head : head + 1, :])


def pairs(target):
    found = []
    for row in range(16):
        for col in range(32):
            to_row, to_col = target(row, col)
            if 0 <= to_row < 16 and 0 <= to_col < 32:
                found.append((row * 32 + col, to_row * 32 + to_col))
    return found


EVERY = ("row", "col")


def device(x, y, z, core):
    return ((z % 8) * 2 + core) * 32 + (x % 4) * 8 + (y % 4) * 2 + z // 8 % 2


FIRST_X, FIRST_Y, FIRST_Z = 2, 2, 9


def apart(place):
    return min(place[0], 4 - place[0]) + min(place[1], 4 - place[1])


PLACES = sorted(
    ((x, y, core) for x in range(4) for y in range(4) for core in (1, 0)),
    key=lambda place: (place != (0, 0, 1), -apart(place)),
)
PLANES = [
    [device(x + FIRST_X, y + FIRST_Y, z, core) for x, y, core in PLACES] for z in range(16)
]
LINES = [
    [device(x, y, z + FIRST_Z, core) for z in range(16)]
    for x in range(4)
    for y in range(4)
    for core in range(2)
]
CHIP_MATE = pairs(lambda row, col: (row ^ 1, col))
FAR_MATE = pairs(lambda row, col: (row, col - 1 if row % 2 else col + 1))
NEXT_CHIP = pairs(lambda row, col: (row + 1 if row % 2 else row - 1, col))
SKIP_CHIP = pairs(lambda row, col: (row - 2 if row % 2 else row + 2, col))


def exchange(array, groups):
    return lax.all_to_all(array, EVERY, 0, 0, axis_index_groups=groups, tiled=True)


def to_all(array, groups):
    return exchange(jnp.broadcast_to(array[None], (len(groups[0]),) + array.shape), groups)


def on_device(features, cotangent, w_qkv, w_out, cos_scale):
    feat = features.reshape(OWN, MODEL)
    cot = cotangent.reshape(OWN, MODEL)
    smem = pl.BlockSpec(memory_space=pltpu.SMEM)

    edge = jax.ShapeDtypeStruct((SENT, MODEL), BF16)
    tile = jnp.concatenate([feat, cot])
    own_edge, mate_message = pl.pallas_call(
        edge_kernel,
        out_shape=(edge, jax.ShapeDtypeStruct((SENT + 144, MODEL), BF16)),
        in_specs=vmem(1),
        out_specs=vmem(2),
        compiler_params=pltpu.CompilerParams(vmem_limit_bytes=2 * 1024 * 1024),
        name="edges",
    )(tile)
    mate = lax.ppermute(mate_message, EVERY, CHIP_MATE)
    other_edge = mate[:SENT]
    far = lax.ppermute(jnp.concatenate([own_edge, other_edge]), EVERY, FAR_MATE)
    key_spots = np.zeros((2, 16, KEYS), np.float32)
    key_spots[:, :2] = TABLES
    key_spots = jnp.asarray(key_spots)
    scales = jnp.broadcast_to(cos_scale[None, :, None], (4, 2, MODEL)).reshape(8, MODEL)
    tile_copy, weights, bias = pl.pallas_call(
        prepare_kernel,
        out_shape=(
            jax.ShapeDtypeStruct((2 * OWN, MODEL), BF16),
            jax.ShapeDtypeStruct((4 * MODEL, MODEL), BF16),
            jax.ShapeDtypeStruct((QUERIES, KEYS), F32),
        ),
        in_specs=vmem(5),
        out_specs=vmem(3),
        compiler_params=pltpu.CompilerParams(vmem_limit_bytes=4 * 1024 * 1024),
        cost_estimate=pl.CostEstimate(
            flops=1000000, bytes_accessed=1 << 20, transcendentals=0
        ),
        name="prepare",
    )(tile, mate, w_qkv, w_out, key_spots)
    next_chip = lax.ppermute(tile_copy, EVERY, NEXT_CHIP)

    far_mate = lax.ppermute(far, EVERY, CHIP_MATE)
    far_next = lax.ppermute(far, EVERY, NEXT_CHIP)
    far_skip = lax.ppermute(far, EVERY, SKIP_CHIP)
    grad_feat, grad_w, scale_tile = pl.pallas_call(
        attention_kernel,
        out_shape=(
            jax.ShapeDtypeStruct((OWN, MODEL), BF16),
            jax.ShapeDtypeStruct((4 * MODEL, MODEL), BF16),
            jax.ShapeDtypeStruct((8, MODEL), BF16),
        ),
        in_specs=vmem(10),
        out_specs=vmem(3),
        scratch_shapes=[
            pltpu.VMEM((KEYS, MODEL), BF16),
            pltpu.VMEM((QUERIES, MODEL), BF16),
            pltpu.VMEM((KEYS, MODEL), BF16),
            pltpu.VMEM((KEYS, MODEL), BF16),
            pltpu.VMEM((QUERIES, MODEL), BF16),
            pltpu.VMEM((QUERIES, MODEL), BF16),
            pltpu.VMEM((2, QUERIES, KEYS), F32),
            pltpu.VMEM((2, QUERIES, KEYS), F32),
            pltpu.VMEM((2, OWN, NEAR), BF16),
            pltpu.VMEM((2, QUERIES, OWN), BF16),
            pltpu.VMEM((2, OWN, NEAR), BF16),
            pltpu.VMEM((2, QUERIES, OWN), BF16),
        ],
        compiler_params=pltpu.CompilerParams(vmem_limit_bytes=16 * 1024 * 1024),
        name="window_attention",
    )(
        scales,
        tile,
        weights,
        mate,
        next_chip,
        far,
        far_skip,
        far_next,
        far_mate,
        bias,
    )

    scale_rows = jnp.broadcast_to(scale_tile[None, None, :2], (SHARES, 1, 2, MODEL))
    shares = jnp.concatenate([grad_w.reshape(SHARES, 8, 2, MODEL), scale_rows], axis=1)
    lane = lax.broadcasted_iota(jnp.int32, (2, MODEL), 1)
    shares, lane = lax.optimization_barrier((shares, lane))
    share = jnp.sum(exchange(shares, PLANES).astype(F32), axis=0)
    term = jnp.sum(jnp.where(lane < 3, share[8], 0.0), axis=1, keepdims=True)
    top = lax.reduce_precision(term, 8, 7)
    middle = lax.reduce_precision(term - top, 8, 7)
    parts = jnp.where(lane == 0, top, jnp.where(lane == 1, middle, term - top - middle))
    parts = jnp.where(lane < 3, parts, 0.0)
    share = jnp.concatenate([share[:8], parts[None]], axis=0).astype(BF16)
    share = jnp.sum(to_all(share, LINES).astype(F32), axis=0)
    share, terms = lax.optimization_barrier((share[:8].astype(BF16).reshape(16, MODEL), share[8]))
    whole = to_all(share, PLANES).reshape(4 * MODEL, MODEL)
    grad_feat, grad_w_qkv, grad_w_out, grad_scale = pl.pallas_call(
        result_kernel,
        out_shape=(
            jax.ShapeDtypeStruct((OWN, MODEL), BF16),
            jax.ShapeDtypeStruct((MODEL, 3 * MODEL), F32),
            jax.ShapeDtypeStruct((MODEL, MODEL), F32),
            jax.ShapeDtypeStruct((2,), F32),
        ),
        in_specs=vmem(3),
        out_specs=vmem(3) + [smem],
        compiler_params=pltpu.CompilerParams(vmem_limit_bytes=2 * 1024 * 1024),
        name="results",
    )(whole, terms, grad_feat)
    return (grad_feat.reshape(ROWS, COLS, MODEL), grad_w_qkv, grad_w_out, grad_scale)


def solution(mesh):
    tokens = P("row", "col", None)
    return jax.shard_map(
        on_device,
        mesh=mesh,
        in_specs=(tokens, tokens, P(), P(), P()),
        out_specs=(tokens, P(), P(), P()),
        check_vma=False,
    )
```

```python
import functools

import jax
import jax.numpy as jnp
import numpy as np
from jax import lax
from jax.experimental import pallas as pl
from jax.experimental.pallas import tpu as pltpu
from jax.sharding import PartitionSpec as P

RADIUS = 3
EPSILON = 1e-06
MODEL = 128
HEAD = 64
ROWS, COLS = 8, 16
OWN = ROWS * COLS
QUERIES = 368
KEYS = 640
NEAR = 384
BLOCK = 16
EDGE = 24
SENT = 80
SHARES = 32
LOG2E = 1.4426950408889634
FAR_AWAY = 1e4

F32 = jnp.float32
BF16 = jnp.bfloat16


def side_columns(left, inner):
    if left:
        return -3 if inner else -6
    return 16 if inner else 19


def token_table(core):
    def tile(holder, start, count, lift):
        token = start + np.arange(count)
        return np.stack([8 * holder + token // 16 + lift, token % 16])

    def edge(holder, left, inner, lift):
        token = np.arange(EDGE)
        row = 8 * holder + token // 3 + lift
        return np.stack([row, token % 3 + side_columns(left, inner)])

    other = 1 - core
    lift = -16 if core == 0 else 16
    left = core == 0
    pieces = [
        tile(core, 0, 128, 0),
        tile(other, 80 * core, 48, 0),
        edge(core, left, True, 0),
        edge(other, left, True, 0),
        edge(other, not left, True, 0),
        edge(core, not left, True, 0),
        tile(other, 80 * other, 48, lift),
        edge(other, not left, True, lift),
        edge(other, left, True, lift),
        tile(other, 48 - 16 * core, 48, 0),
        edge(core, left, False, 0),
        edge(other, left, False, 0),
        edge(other, not left, False, 0),
        edge(core, not left, False, 0),
        tile(other, 48 - 16 * other, 48, lift),
        edge(other, not left, False, lift),
        edge(other, left, False, lift),
        np.full((2, 32), FAR_AWAY),
    ]
    return np.concatenate(pieces, axis=1).astype(np.float32)


TABLES = np.stack([token_table(0), token_table(1)])


def vmem(count):
    return [pl.BlockSpec(memory_space=pltpu.VMEM)] * count


def dot_nt(left, right):
    return lax.dot_general(
        left, right, (((1,), (1,)), ((), ())), preferred_element_type=F32
    )


def dot_tn(left, right):
    return lax.dot_general(
        left, right, (((0,), (0,)), ((), ())), preferred_element_type=F32
    )


def dot_nn(left, right):
    return jnp.dot(left, right, preferred_element_type=F32)


def edge_kernel(tile, own_edge, mate_message):
    core, _, _ = place_here()
    spot = lax.broadcasted_iota(jnp.int32, (SENT, 128), 0)
    token = lax.broadcasted_iota(jnp.int32, (SENT, 128), 1)
    kind = jnp.where(spot >= EDGE, 1, 0) + jnp.where(spot >= 2 * EDGE, 1, 0)
    index = spot - EDGE * kind
    row = (index * 43) >> 7
    step = index - 3 * row
    outer = kind == 1
    right = row * 16 + step + jnp.where(outer, 10, 13)
    left = row * 16 + step + jnp.where(outer, 3, 0)
    used = spot < 3 * EDGE
    from_cot = kind == 2
    for ref, wanted in (
        (own_edge, jnp.where(core == 0, right, left)),
        (mate_message, jnp.where(core == 0, left, right)),
    ):
        hit = (wanted == token) & used
        of_feat = jnp.where(hit & ~from_cot, 1.0, 0.0).astype(BF16)
        of_cot = jnp.where(hit & from_cot, 1.0, 0.0).astype(BF16)
        ref[0:SENT, :] = (
            dot_nn(of_feat, tile[0:OWN, :]) + dot_nn(of_cot, tile[OWN:, :])
        ).astype(BF16)
    half = 1 - core
    mate_message[SENT : SENT + 48, :] = rows_at(tile, 80 * half, 48)
    mate_message[SENT + 48 : SENT + 96, :] = rows_at(tile, 48 - 16 * half, 48)
    mate_message[SENT + 96 : SENT + 144, :] = rows_at(tile, OWN + 80 * half, 48)


def place_here():
    row, col = lax.axis_index("row"), lax.axis_index("col")
    return row & 1, (row >> 1) * 16, col * 16


def rows_at(ref, start, count):
    return ref[pl.ds(pl.multiple_of(start, 16), count), :]


def prepare_kernel(
    tile, mate, w_qkv, w_out, key_spots, tile_copy, weights, bias, near_kv, near_q, near_d
):
    tile_copy[...] = tile[...]
    for part in range(3):
        columns = slice(part * MODEL, (part + 1) * MODEL)
        weights[columns, :] = w_qkv[:, columns]
    weights[3 * MODEL :, :] = w_out[...]
    near = jnp.concatenate([tile[0:OWN, :], mate[SENT : SENT + 96, :]], axis=0)
    near_kv[...] = dot_nn(near, w_qkv[:, MODEL:]).astype(BF16)
    near_q[...] = dot_nn(near[:176], w_qkv[:, :MODEL]).astype(BF16)
    near_cots = jnp.concatenate([tile[OWN:, :], mate[SENT + 96 : SENT + 144, :]], axis=0)
    near_d[...] = dot_nt(near_cots, w_out[...]).astype(BF16)

    core, first_row, first_col = place_here()
    spots = jnp.where(core == 0, key_spots[0], key_spots[1])
    key_rows, key_cols = spots[0:1, :], spots[1:2, :]
    turn = lax.broadcasted_iota(jnp.int32, (16, MODEL), 0)
    turn = jnp.where(turn == lax.broadcasted_iota(jnp.int32, (16, MODEL), 1), 1.0, 0.0)
    query_spots = dot_tn(spots[:, :NEAR].astype(BF16), turn.astype(BF16))
    all_rows = key_rows + first_row.astype(F32)
    all_cols = key_cols + first_col.astype(F32)
    inside = (all_rows >= 0) & (all_rows < 128) & (all_cols >= 0) & (all_cols < 512)
    key_rows = jnp.where(inside, key_rows, FAR_AWAY)
    for start in range(0, QUERIES, BLOCK):
        here = query_spots[start : start + BLOCK, :]
        apart = jnp.maximum(
            jnp.abs(here[:, 0:1] - key_rows), jnp.abs(here[:, 1:2] - key_cols)
        )
        bias[start : start + BLOCK, :] = jnp.where(apart <= RADIUS, 0.0, -1e30)


def attention_kernel(
    scales,
    tile,
    weights,
    near_kv,
    near_q,
    near_d,
    next_chip,
    far,
    far_skip,
    far_next,
    far_mate,
    bias,
    grad_feat,
    grad_w,
    grad_scale,
    tokens,
    cots,
    keys,
    values,
    queries,
    d_attn,
    raw,
    dots,
    mix_own,
    mix_key,
    slope_own,
    slope_key,
):
    core, _, _ = place_here()
    other = 1 - core
    w_query, w_key, w_value, w_out = (
        weights[start : start + MODEL, :] for start in range(0, 4 * MODEL, MODEL)
    )
    far_wide = far[...].astype(F32)
    mate_wide = far_mate[...].astype(F32)
    next_wide = far_next[0:SENT, :].astype(F32)
    skip_wide = far_skip[SENT:, :].astype(F32)
    edges = (
        far_wide[:SENT],
        far_wide[SENT:],
        mate_wide[:SENT],
        mate_wide[SENT:],
        next_wide,
        skip_wide,
    )

    def strip(kind, chosen):
        pieces = [edge[kind * EDGE : (kind + 1) * EDGE] for edge in chosen]
        return jnp.concatenate(pieces, axis=0).astype(BF16)

    tokens[176:272, :] = strip(0, edges[:4])
    tokens[272:320, :] = rows_at(next_chip, 80 * other, 48)
    tokens[320:368, :] = strip(0, edges[4:])
    tokens[416:512, :] = strip(1, edges[:4])
    tokens[512:560, :] = rows_at(next_chip, 48 - 16 * other, 48)
    tokens[560:608, :] = strip(1, edges[4:])
    tokens[608:640, :] = jnp.zeros((32, MODEL), BF16)
    cots[176:272, :] = strip(2, edges[:4])
    cots[272:320, :] = rows_at(next_chip, OWN + 80 * other, 48)
    cots[320:368, :] = strip(2, edges[4:])

    w_both = jnp.concatenate([w_key, w_value], axis=1)
    for rows, projected in (
        (slice(0, 176), near_kv[0:176, :]),
        (slice(368, 416), near_kv[176:224, :]),
        (slice(176, 368), dot_nn(tokens[176:368, :], w_both).astype(BF16)),
        (slice(416, KEYS), dot_nn(tokens[416:KEYS, :], w_both).astype(BF16)),
    ):
        keys[rows, :] = projected[:, :MODEL]
        values[rows, :] = projected[:, MODEL:]
    queries[0:176, :] = near_q[...]
    queries[176:QUERIES, :] = dot_nn(tokens[176:QUERIES, :], w_query).astype(BF16)
    d_attn[0:176, :] = near_d[...]
    d_attn[176:QUERIES, :] = dot_nt(cots[176:QUERIES, :], w_out).astype(BF16)

    key_wide = keys[...].astype(F32)
    square = key_wide * key_wide
    upper = square.astype(BF16)
    lower = (square - upper.astype(F32)).astype(BF16)
    head_of = lax.broadcasted_iota(jnp.int32, (16, MODEL), 1) // HEAD
    picks = jnp.where(
        head_of == lax.broadcasted_iota(jnp.int32, (16, MODEL), 0), 1.0, 0.0
    ).astype(BF16)
    key_inverse = lax.rsqrt(dot_nt(picks, upper) + dot_nt(picks, lower) + EPSILON)

    first = lax.broadcasted_iota(jnp.int32, (1, MODEL), 1) < HEAD

    def head_sums(array):
        low = jnp.sum(jnp.where(first, array, 0.0), axis=1, keepdims=True)
        high = jnp.sum(jnp.where(first, 0.0, array), axis=1, keepdims=True)
        return low, high

    for head in range(2):
        own_lanes = first if head == 0 else ~first
        for rows, width in ((slice(0, OWN), NEAR), (slice(OWN, QUERIES), KEYS)):
            query = jnp.where(own_lanes, queries[rows, :], 0.0).astype(BF16)
            grad = jnp.where(own_lanes, d_attn[rows, :], 0.0).astype(BF16)
            raw[head, rows, :width] = dot_nt(query, keys[0:width, :])
            dots[head, rows, :width] = dot_nt(grad, values[0:width, :])

    key_inv = [key_inverse[head : head + 1, :] for head in range(2)]
    wide = jnp.concatenate([scales[...]] * (KEYS // MODEL), axis=1)
    key_reach = [key_inv[head] * wide[head : head + 1, :] for head in range(2)]
    scale_lanes = jnp.where(first, scales[0:1, :], scales[1:2, :])
    scale_sums = [jnp.zeros((BLOCK, 1), F32), jnp.zeros((BLOCK, 1), F32)]
    for start in range(0, QUERIES, BLOCK):
        rows = slice(start, start + BLOCK)
        width = NEAR if start < OWN else KEYS
        query_wide = queries[rows, :].astype(F32)
        norms = head_sums(query_wide * query_wide)
        for head in range(2):
            inverse = lax.rsqrt(norms[head] + EPSILON)
            score = raw[head, rows, :width] * (inverse * LOG2E) * key_reach[head][:, :width]
            expo = jnp.exp2(score + bias[rows, :width])
            gain = dots[head, rows, :width]
            share = 1.0 / (jnp.sum(expo, axis=1, keepdims=True) + 1e-30)
            center = jnp.sum(expo * gain, axis=1, keepdims=True) * share
            if start < OWN:
                weight = expo[:, :NEAR] * share
                slope = weight * (gain[:, :NEAR] - center)
                pull = slope * key_inv[head][:, :NEAR]
                scale_sums[head] += inverse * jnp.sum(
                    pull * raw[head, rows, :NEAR], axis=1, keepdims=True
                )
                mix_own[head, rows, :] = weight.astype(BF16)
                slope_own[head, rows, :] = pull.astype(BF16)
                weight = weight[:, :OWN]
                slope = slope[:, :OWN]
            else:
                weight = expo[:, :OWN] * share
                slope = weight * (gain[:, :OWN] - center)
            mix_key[head, rows, :] = weight.astype(BF16)
            slope_key[head, rows, :] = (slope * inverse).astype(BF16)

    def both(dot, left, right):
        return jnp.where(first, dot(left[0], right), dot(left[1], right))

    attn_out = both(dot_nn, mix_own, values[0:NEAR, :]).astype(BF16)
    dq_unit = scale_lanes * both(dot_nn, slope_own, keys[0:NEAR, :])
    dk_unit = scale_lanes * both(dot_tn, slope_key, queries[...])
    dv = both(dot_tn, mix_key, d_attn[...])

    def unit_backward(vector, grad_unit):
        low, high = head_sums(vector * vector)
        inverse = jnp.where(first, lax.rsqrt(low + EPSILON), lax.rsqrt(high + EPSILON))
        unit = vector * inverse
        low, high = head_sums(unit * grad_unit)
        return (grad_unit - unit * jnp.where(first, low, high)) * inverse

    dq = unit_backward(queries[0:OWN, :].astype(F32), dq_unit).astype(BF16)
    dk = unit_backward(keys[0:OWN, :].astype(F32), dk_unit).astype(BF16)
    dv = dv.astype(BF16)
    grad_feat[...] = (
        dot_nt(dq, w_query)
        + dot_nt(dk, w_key)
        + dot_nt(dv, w_value)
    ).astype(BF16)
    norm = 1.0 / 256.0
    for part, grad in enumerate((dq, dk, dv)):
        grad_w[part * MODEL : (part + 1) * MODEL, :] = (
            dot_tn(tile[0:OWN, :], grad) * norm
        ).astype(BF16)
    grad_w[3 * MODEL :, :] = (dot_tn(attn_out, tile[OWN:, :]) * norm).astype(BF16)

    lane = lax.broadcasted_iota(jnp.int32, (8, MODEL), 1)
    part = lax.broadcasted_iota(jnp.int32, (8, MODEL), 0)
    terms = [jnp.sum(total, axis=0, keepdims=True) * norm for total in scale_sums]
    rest = jnp.where(part == 0, terms[0], terms[1])
    held = jnp.zeros((8, MODEL), F32)
    for which in range(3):
        piece = rest.astype(BF16).astype(F32)
        held = jnp.where(lane == which, piece, held)
        rest = rest - piece
    grad_scale[...] = held.astype(BF16)


def result_kernel(whole, terms, feat_tile, grad_feat, grad_w_qkv, grad_w_out, grad_scale):
    grad_feat[...] = feat_tile[...]
    for part in range(3):
        rows = slice(part * MODEL, (part + 1) * MODEL)
        grad_w_qkv[:, rows] = whole[rows, :].astype(F32)
    grad_w_out[...] = whole[3 * MODEL :, :].astype(F32)
    for head in range(2):
        grad_scale[head] = jnp.sum(terms[head : head + 1, :])


def pairs(target):
    found = []
    for row in range(16):
        for col in range(32):
            to_row, to_col = target(row, col)
            if 0 <= to_row < 16 and 0 <= to_col < 32:
                found.append((row * 32 + col, to_row * 32 + to_col))
    return found


EVERY = ("row", "col")


def device(x, y, z, core):
    return ((z % 8) * 2 + core) * 32 + (x % 4) * 8 + (y % 4) * 2 + z // 8 % 2


FIRST_X, FIRST_Y, FIRST_Z = 2, 2, 9


def apart(place):
    return min(place[0], 4 - place[0]) + min(place[1], 4 - place[1])


PLACES = sorted(
    ((x, y, core) for x in range(4) for y in range(4) for core in (1, 0)),
    key=lambda place: (place != (0, 0, 1), -apart(place)),
)
PLANES = [
    [device(x + FIRST_X, y + FIRST_Y, z, core) for x, y, core in PLACES] for z in range(16)
]
LINES = [
    [device(x, y, z + FIRST_Z, core) for z in range(16)]
    for x in range(4)
    for y in range(4)
    for core in range(2)
]
CHIP_MATE = pairs(lambda row, col: (row ^ 1, col))
FAR_MATE = pairs(lambda row, col: (row, col - 1 if row % 2 else col + 1))
NEXT_CHIP = pairs(lambda row, col: (row + 1 if row % 2 else row - 1, col))
SKIP_CHIP = pairs(lambda row, col: (row - 2 if row % 2 else row + 2, col))


def exchange(array, groups):
    return lax.all_to_all(array, EVERY, 0, 0, axis_index_groups=groups, tiled=True)


def to_all(array, groups):
    return exchange(jnp.broadcast_to(array[None], (len(groups[0]),) + array.shape), groups)


def on_device(features, cotangent, w_qkv, w_out, cos_scale):
    feat = features.reshape(OWN, MODEL)
    cot = cotangent.reshape(OWN, MODEL)
    smem = pl.BlockSpec(memory_space=pltpu.SMEM)

    edge = jax.ShapeDtypeStruct((SENT, MODEL), BF16)
    tile = jnp.concatenate([feat, cot])
    own_edge, mate_message = pl.pallas_call(
        edge_kernel,
        out_shape=(edge, jax.ShapeDtypeStruct((SENT + 144, MODEL), BF16)),
        in_specs=vmem(1),
        out_specs=vmem(2),
        compiler_params=pltpu.CompilerParams(vmem_limit_bytes=2 * 1024 * 1024),
        name="edges",
    )(tile)
    mate = lax.ppermute(mate_message, EVERY, CHIP_MATE)
    other_edge = mate[:SENT]
    far = lax.ppermute(jnp.concatenate([own_edge, other_edge]), EVERY, FAR_MATE)
    key_spots = np.zeros((2, 16, KEYS), np.float32)
    key_spots[:, :2] = TABLES
    key_spots = jnp.asarray(key_spots)
    scales = jnp.broadcast_to(cos_scale[None, :, None], (4, 2, MODEL)).reshape(8, MODEL)
    tile_copy, weights, bias, near_kv, near_q, near_d = pl.pallas_call(
        prepare_kernel,
        out_shape=(
            jax.ShapeDtypeStruct((2 * OWN, MODEL), BF16),
            jax.ShapeDtypeStruct((4 * MODEL, MODEL), BF16),
            jax.ShapeDtypeStruct((QUERIES, KEYS), F32),
            jax.ShapeDtypeStruct((224, 2 * MODEL), BF16),
            jax.ShapeDtypeStruct((176, MODEL), BF16),
            jax.ShapeDtypeStruct((176, MODEL), BF16),
        ),
        in_specs=vmem(5),
        out_specs=vmem(6),
        compiler_params=pltpu.CompilerParams(vmem_limit_bytes=4 * 1024 * 1024),
        cost_estimate=pl.CostEstimate(
            flops=1000000, bytes_accessed=1 << 20, transcendentals=0
        ),
        name="prepare",
    )(tile, mate, w_qkv, w_out, key_spots)
    next_chip = lax.ppermute(tile_copy, EVERY, NEXT_CHIP)

    far_mate = lax.ppermute(far, EVERY, CHIP_MATE)
    far_next = lax.ppermute(far, EVERY, NEXT_CHIP)
    far_skip = lax.ppermute(far, EVERY, SKIP_CHIP)
    grad_feat, grad_w, scale_tile = pl.pallas_call(
        attention_kernel,
        out_shape=(
            jax.ShapeDtypeStruct((OWN, MODEL), BF16),
            jax.ShapeDtypeStruct((4 * MODEL, MODEL), BF16),
            jax.ShapeDtypeStruct((8, MODEL), BF16),
        ),
        in_specs=vmem(12),
        out_specs=vmem(3),
        scratch_shapes=[
            pltpu.VMEM((KEYS, MODEL), BF16),
            pltpu.VMEM((QUERIES, MODEL), BF16),
            pltpu.VMEM((KEYS, MODEL), BF16),
            pltpu.VMEM((KEYS, MODEL), BF16),
            pltpu.VMEM((QUERIES, MODEL), BF16),
            pltpu.VMEM((QUERIES, MODEL), BF16),
            pltpu.VMEM((2, QUERIES, KEYS), F32),
            pltpu.VMEM((2, QUERIES, KEYS), F32),
            pltpu.VMEM((2, OWN, NEAR), BF16),
            pltpu.VMEM((2, QUERIES, OWN), BF16),
            pltpu.VMEM((2, OWN, NEAR), BF16),
            pltpu.VMEM((2, QUERIES, OWN), BF16),
        ],
        compiler_params=pltpu.CompilerParams(vmem_limit_bytes=16 * 1024 * 1024),
        name="window_attention",
    )(
        scales,
        tile,
        weights,
        near_kv,
        near_q,
        near_d,
        next_chip,
        far,
        far_skip,
        far_next,
        far_mate,
        bias,
    )

    scale_rows = jnp.broadcast_to(scale_tile[None, None, :2], (SHARES, 1, 2, MODEL))
    shares = jnp.concatenate([grad_w.reshape(SHARES, 8, 2, MODEL), scale_rows], axis=1)
    lane = lax.broadcasted_iota(jnp.int32, (2, MODEL), 1)
    shares, lane = lax.optimization_barrier((shares, lane))
    share = jnp.sum(exchange(shares, PLANES).astype(F32), axis=0)
    term = jnp.sum(jnp.where(lane < 3, share[8], 0.0), axis=1, keepdims=True)
    top = lax.reduce_precision(term, 8, 7)
    middle = lax.reduce_precision(term - top, 8, 7)
    parts = jnp.where(lane == 0, top, jnp.where(lane == 1, middle, term - top - middle))
    parts = jnp.where(lane < 3, parts, 0.0)
    share = jnp.concatenate([share[:8], parts[None]], axis=0).astype(BF16)
    share = jnp.sum(to_all(share, LINES).astype(F32), axis=0)
    share, terms = lax.optimization_barrier((share[:8].astype(BF16).reshape(16, MODEL), share[8]))
    whole = to_all(share, PLANES).reshape(4 * MODEL, MODEL)
    grad_feat, grad_w_qkv, grad_w_out, grad_scale = pl.pallas_call(
        result_kernel,
        out_shape=(
            jax.ShapeDtypeStruct((OWN, MODEL), BF16),
            jax.ShapeDtypeStruct((MODEL, 3 * MODEL), F32),
            jax.ShapeDtypeStruct((MODEL, MODEL), F32),
            jax.ShapeDtypeStruct((2,), F32),
        ),
        in_specs=vmem(3),
        out_specs=vmem(3) + [smem],
        compiler_params=pltpu.CompilerParams(vmem_limit_bytes=2 * 1024 * 1024),
        name="results",
    )(whole, terms, grad_feat)
    return (grad_feat.reshape(ROWS, COLS, MODEL), grad_w_qkv, grad_w_out, grad_scale)


def solution(mesh):
    tokens = P("row", "col", None)
    return jax.shard_map(
        on_device,
        mesh=mesh,
        in_specs=(tokens, tokens, P(), P(), P()),
        out_specs=(tokens, P(), P(), P()),
        check_vma=False,
    )
```

```python
import functools

import jax
import jax.numpy as jnp
import numpy as np
from jax import lax
from jax.experimental import pallas as pl
from jax.experimental.pallas import tpu as pltpu
from jax.sharding import PartitionSpec as P

RADIUS = 3
EPSILON = 1e-06
MODEL = 128
HEAD = 64
ROWS, COLS = 8, 16
OWN = ROWS * COLS
QUERIES = 368
KEYS = 640
NEAR = 384
BLOCK = 16
EDGE = 24
SENT = 80
SHARES = 32
LOG2E = 1.4426950408889634
FAR_AWAY = 1e4

F32 = jnp.float32
BF16 = jnp.bfloat16


def side_columns(left, inner):
    if left:
        return -3 if inner else -6
    return 16 if inner else 19


def token_table(core):
    def tile(holder, start, count, lift):
        token = start + np.arange(count)
        return np.stack([8 * holder + token // 16 + lift, token % 16])

    def edge(holder, left, inner, lift):
        token = np.arange(EDGE)
        row = 8 * holder + token // 3 + lift
        return np.stack([row, token % 3 + side_columns(left, inner)])

    other = 1 - core
    lift = -16 if core == 0 else 16
    left = core == 0
    pieces = [
        tile(core, 0, 128, 0),
        tile(other, 80 * core, 48, 0),
        edge(core, left, True, 0),
        edge(other, left, True, 0),
        edge(other, not left, True, 0),
        edge(core, not left, True, 0),
        tile(other, 80 * other, 48, lift),
        edge(other, not left, True, lift),
        edge(other, left, True, lift),
        tile(other, 48 - 16 * core, 48, 0),
        edge(core, left, False, 0),
        edge(other, left, False, 0),
        edge(other, not left, False, 0),
        edge(core, not left, False, 0),
        tile(other, 48 - 16 * other, 48, lift),
        edge(other, not left, False, lift),
        edge(other, left, False, lift),
        np.full((2, 32), FAR_AWAY),
    ]
    return np.concatenate(pieces, axis=1).astype(np.float32)


TABLES = np.stack([token_table(0), token_table(1)])


def vmem(count):
    return [pl.BlockSpec(memory_space=pltpu.VMEM)] * count


def dot_nt(left, right):
    return lax.dot_general(
        left, right, (((1,), (1,)), ((), ())), preferred_element_type=F32
    )


def dot_tn(left, right):
    return lax.dot_general(
        left, right, (((0,), (0,)), ((), ())), preferred_element_type=F32
    )


def dot_nn(left, right):
    return jnp.dot(left, right, preferred_element_type=F32)


def edge_kernel(tile, own_edge, mate_message):
    core, _, _ = place_here()
    spot = lax.broadcasted_iota(jnp.int32, (SENT, 128), 0)
    token = lax.broadcasted_iota(jnp.int32, (SENT, 128), 1)
    kind = jnp.where(spot >= EDGE, 1, 0) + jnp.where(spot >= 2 * EDGE, 1, 0)
    index = spot - EDGE * kind
    row = (index * 43) >> 7
    step = index - 3 * row
    outer = kind == 1
    right = row * 16 + step + jnp.where(outer, 10, 13)
    left = row * 16 + step + jnp.where(outer, 3, 0)
    used = spot < 3 * EDGE
    from_cot = kind == 2
    for ref, wanted in (
        (own_edge, jnp.where(core == 0, right, left)),
        (mate_message, jnp.where(core == 0, left, right)),
    ):
        hit = (wanted == token) & used
        of_feat = jnp.where(hit & ~from_cot, 1.0, 0.0).astype(BF16)
        of_cot = jnp.where(hit & from_cot, 1.0, 0.0).astype(BF16)
        ref[0:SENT, :] = (
            dot_nn(of_feat, tile[0:OWN, :]) + dot_nn(of_cot, tile[OWN:, :])
        ).astype(BF16)
    half = 1 - core
    mate_message[SENT : SENT + 48, :] = rows_at(tile, 80 * half, 48)
    mate_message[SENT + 48 : SENT + 96, :] = rows_at(tile, 48 - 16 * half, 48)
    mate_message[SENT + 96 : SENT + 144, :] = rows_at(tile, OWN + 80 * half, 48)


def place_here():
    row, col = lax.axis_index("row"), lax.axis_index("col")
    return row & 1, (row >> 1) * 16, col * 16


def rows_at(ref, start, count):
    return ref[pl.ds(pl.multiple_of(start, 16), count), :]


def prepare_kernel(
    tile, mate, w_qkv, w_out, key_spots, tile_copy, weights, bias, near_kv, near_q, near_d
):
    tile_copy[...] = tile[...]
    for part in range(3):
        columns = slice(part * MODEL, (part + 1) * MODEL)
        weights[columns, :] = w_qkv[:, columns]
    weights[3 * MODEL :, :] = w_out[...]
    near = jnp.concatenate([tile[0:OWN, :], mate[SENT : SENT + 96, :]], axis=0)
    near_kv[...] = dot_nn(near, w_qkv[:, MODEL:]).astype(BF16)
    near_q[...] = dot_nn(near[:176], w_qkv[:, :MODEL]).astype(BF16)
    near_cots = jnp.concatenate([tile[OWN:, :], mate[SENT + 96 : SENT + 144, :]], axis=0)
    near_d[...] = dot_nt(near_cots, w_out[...]).astype(BF16)

    core, first_row, first_col = place_here()
    spots = jnp.where(core == 0, key_spots[0], key_spots[1])
    key_rows, key_cols = spots[0:1, :], spots[1:2, :]
    turn = lax.broadcasted_iota(jnp.int32, (16, MODEL), 0)
    turn = jnp.where(turn == lax.broadcasted_iota(jnp.int32, (16, MODEL), 1), 1.0, 0.0)
    query_spots = dot_tn(spots[:, :NEAR].astype(BF16), turn.astype(BF16))
    all_rows = key_rows + first_row.astype(F32)
    all_cols = key_cols + first_col.astype(F32)
    inside = (all_rows >= 0) & (all_rows < 128) & (all_cols >= 0) & (all_cols < 512)
    key_rows = jnp.where(inside, key_rows, FAR_AWAY)
    for start in range(0, QUERIES, BLOCK):
        here = query_spots[start : start + BLOCK, :]
        apart = jnp.maximum(
            jnp.abs(here[:, 0:1] - key_rows), jnp.abs(here[:, 1:2] - key_cols)
        )
        bias[start : start + BLOCK, :] = jnp.where(apart <= RADIUS, 0.0, -1e30)


def attention_kernel(
    scales,
    tile,
    weights,
    near_kv,
    near_q,
    near_d,
    next_chip,
    far,
    far_skip,
    far_next,
    far_mate,
    bias,
    grad_feat,
    grad_w,
    grad_scale,
    tokens,
    cots,
    keys,
    values,
    queries,
    d_attn,
    raw,
    dots,
    mix_own,
    mix_key,
    slope_own,
    slope_key,
):
    core, _, _ = place_here()
    other = 1 - core
    w_query, w_key, w_value, w_out = (
        weights[start : start + MODEL, :] for start in range(0, 4 * MODEL, MODEL)
    )
    far_wide = far[...].astype(F32)
    mate_wide = far_mate[...].astype(F32)
    next_wide = far_next[0:SENT, :].astype(F32)
    skip_wide = far_skip[SENT:, :].astype(F32)
    edges = (
        far_wide[:SENT],
        far_wide[SENT:],
        mate_wide[:SENT],
        mate_wide[SENT:],
        next_wide,
        skip_wide,
    )

    def strip(kind, chosen):
        pieces = [edge[kind * EDGE : (kind + 1) * EDGE] for edge in chosen]
        return jnp.concatenate(pieces, axis=0).astype(BF16)

    tokens[176:272, :] = strip(0, edges[:4])
    tokens[272:320, :] = rows_at(next_chip, 80 * other, 48)
    tokens[320:368, :] = strip(0, edges[4:])
    tokens[416:512, :] = strip(1, edges[:4])
    tokens[512:560, :] = rows_at(next_chip, 48 - 16 * other, 48)
    tokens[560:608, :] = strip(1, edges[4:])
    tokens[608:640, :] = jnp.zeros((32, MODEL), BF16)
    cots[176:272, :] = strip(2, edges[:4])
    cots[272:320, :] = rows_at(next_chip, OWN + 80 * other, 48)
    cots[320:368, :] = strip(2, edges[4:])

    w_both = jnp.concatenate([w_key, w_value], axis=1)
    for rows, projected in (
        (slice(0, 176), near_kv[0:176, :]),
        (slice(368, 416), near_kv[176:224, :]),
        (slice(176, 368), dot_nn(tokens[176:368, :], w_both).astype(BF16)),
        (slice(416, KEYS), dot_nn(tokens[416:KEYS, :], w_both).astype(BF16)),
    ):
        keys[rows, :] = projected[:, :MODEL]
        values[rows, :] = projected[:, MODEL:]
    queries[0:176, :] = near_q[...]
    queries[176:QUERIES, :] = dot_nn(tokens[176:QUERIES, :], w_query).astype(BF16)
    d_attn[0:176, :] = near_d[...]
    d_attn[176:QUERIES, :] = dot_nt(cots[176:QUERIES, :], w_out).astype(BF16)

    key_wide = keys[...].astype(F32)
    square = key_wide * key_wide
    upper = square.astype(BF16)
    lower = (square - upper.astype(F32)).astype(BF16)
    head_of = lax.broadcasted_iota(jnp.int32, (16, MODEL), 1) // HEAD
    picks = jnp.where(
        head_of == lax.broadcasted_iota(jnp.int32, (16, MODEL), 0), 1.0, 0.0
    ).astype(BF16)
    key_inverse = lax.rsqrt(dot_nt(picks, upper) + dot_nt(picks, lower) + EPSILON)

    first = lax.broadcasted_iota(jnp.int32, (1, MODEL), 1) < HEAD

    def head_sums(array):
        low = jnp.sum(jnp.where(first, array, 0.0), axis=1, keepdims=True)
        high = jnp.sum(jnp.where(first, 0.0, array), axis=1, keepdims=True)
        return low, high

    for head in range(2):
        own_lanes = first if head == 0 else ~first
        for rows, width in ((slice(0, OWN), NEAR), (slice(OWN, QUERIES), KEYS)):
            query = jnp.where(own_lanes, queries[rows, :], 0.0).astype(BF16)
            grad = jnp.where(own_lanes, d_attn[rows, :], 0.0).astype(BF16)
            raw[head, rows, :width] = dot_nt(query, keys[0:width, :])
            dots[head, rows, :width] = dot_nt(grad, values[0:width, :])

    key_inv = [key_inverse[head : head + 1, :] for head in range(2)]
    wide = jnp.concatenate([scales[...]] * (KEYS // MODEL), axis=1)
    key_reach = [key_inv[head] * wide[head : head + 1, :] for head in range(2)]
    scale_lanes = jnp.where(first, scales[0:1, :], scales[1:2, :])
    scale_sums = [jnp.zeros((BLOCK, 1), F32), jnp.zeros((BLOCK, 1), F32)]
    for start in range(0, QUERIES, BLOCK):
        rows = slice(start, start + BLOCK)
        width = NEAR if start < OWN else KEYS
        query_wide = queries[rows, :].astype(F32)
        norms = head_sums(query_wide * query_wide)
        for head in range(2):
            inverse = lax.rsqrt(norms[head] + EPSILON)
            score = raw[head, rows, :width] * (inverse * LOG2E) * key_reach[head][:, :width]
            expo = jnp.exp2(score + bias[rows, :width])
            gain = dots[head, rows, :width]
            share = 1.0 / (jnp.sum(expo, axis=1, keepdims=True) + 1e-30)
            center = jnp.sum(expo * gain, axis=1, keepdims=True) * share
            if start < OWN:
                weight = expo[:, :NEAR] * share
                slope = weight * (gain[:, :NEAR] - center)
                pull = slope * key_inv[head][:, :NEAR]
                scale_sums[head] += inverse * jnp.sum(
                    pull * raw[head, rows, :NEAR], axis=1, keepdims=True
                )
                mix_own[head, rows, :] = weight.astype(BF16)
                slope_own[head, rows, :] = pull.astype(BF16)
                weight = weight[:, :OWN]
                slope = slope[:, :OWN]
            else:
                weight = expo[:, :OWN] * share
                slope = weight * (gain[:, :OWN] - center)
            mix_key[head, rows, :] = weight.astype(BF16)
            slope_key[head, rows, :] = (slope * inverse).astype(BF16)

    def both(dot, left, right):
        return jnp.where(first, dot(left[0], right), dot(left[1], right))

    attn_out = both(dot_nn, mix_own, values[0:NEAR, :]).astype(BF16)
    dq_unit = scale_lanes * both(dot_nn, slope_own, keys[0:NEAR, :])
    dk_unit = scale_lanes * both(dot_tn, slope_key, queries[...])
    dv = both(dot_tn, mix_key, d_attn[...])

    def unit_backward(vector, grad_unit):
        low, high = head_sums(vector * vector)
        inverse = jnp.where(first, lax.rsqrt(low + EPSILON), lax.rsqrt(high + EPSILON))
        unit = vector * inverse
        low, high = head_sums(unit * grad_unit)
        return (grad_unit - unit * jnp.where(first, low, high)) * inverse

    dq = unit_backward(queries[0:OWN, :].astype(F32), dq_unit).astype(BF16)
    dk = unit_backward(keys[0:OWN, :].astype(F32), dk_unit).astype(BF16)
    dv = dv.astype(BF16)
    grad_feat[...] = (
        dot_nt(dq, w_query)
        + dot_nt(dk, w_key)
        + dot_nt(dv, w_value)
    ).astype(BF16)
    norm = 1.0 / 256.0
    for part, grad in enumerate((dq, dk, dv)):
        grad_w[part * MODEL : (part + 1) * MODEL, :] = (
            dot_tn(tile[0:OWN, :], grad) * norm
        ).astype(BF16)
    grad_w[3 * MODEL :, :] = (dot_tn(attn_out, tile[OWN:, :]) * norm).astype(BF16)

    lane = lax.broadcasted_iota(jnp.int32, (8, MODEL), 1)
    part = lax.broadcasted_iota(jnp.int32, (8, MODEL), 0)
    terms = [jnp.sum(total, axis=0, keepdims=True) * norm for total in scale_sums]
    rest = jnp.where(part == 0, terms[0], terms[1])
    held = jnp.zeros((8, MODEL), F32)
    for which in range(3):
        piece = rest.astype(BF16).astype(F32)
        held = jnp.where(lane == which, piece, held)
        rest = rest - piece
    grad_scale[...] = held.astype(BF16)


def result_kernel(whole, terms, feat_tile, grad_feat, grad_w_qkv, grad_w_out, grad_scale):
    grad_feat[...] = feat_tile[...]
    for part in range(3):
        rows = slice(part * MODEL, (part + 1) * MODEL)
        grad_w_qkv[:, rows] = whole[rows, :].astype(F32)
    grad_w_out[...] = whole[3 * MODEL :, :].astype(F32)
    for head in range(2):
        grad_scale[head] = jnp.sum(terms[head : head + 1, :])


def pairs(target):
    found = []
    for row in range(16):
        for col in range(32):
            to_row, to_col = target(row, col)
            if 0 <= to_row < 16 and 0 <= to_col < 32:
                found.append((row * 32 + col, to_row * 32 + to_col))
    return found


EVERY = ("row", "col")


def device(x, y, z, core):
    return ((z % 8) * 2 + core) * 32 + (x % 4) * 8 + (y % 4) * 2 + z // 8 % 2


FIRST_X, FIRST_Y, FIRST_Z = 2, 2, 9


def apart(place):
    return min(place[0], 4 - place[0]) + min(place[1], 4 - place[1])


PLACES = sorted(
    ((x, y, core) for x in range(4) for y in range(4) for core in (1, 0)),
    key=lambda place: (place != (0, 0, 1), -apart(place)),
)
PLANES = [
    [device(x + FIRST_X, y + FIRST_Y, z, core) for x, y, core in PLACES] for z in range(16)
]
LINES = [
    [device(x, y, z + FIRST_Z - core, core) for z in range(16)]
    for x in range(4)
    for y in range(4)
    for core in range(2)
]
CHIP_MATE = pairs(lambda row, col: (row ^ 1, col))
FAR_MATE = pairs(lambda row, col: (row, col - 1 if row % 2 else col + 1))
NEXT_CHIP = pairs(lambda row, col: (row + 1 if row % 2 else row - 1, col))
SKIP_CHIP = pairs(lambda row, col: (row - 2 if row % 2 else row + 2, col))


def exchange(array, groups):
    return lax.all_to_all(array, EVERY, 0, 0, axis_index_groups=groups, tiled=True)


def to_all(array, groups):
    return exchange(jnp.broadcast_to(array[None], (len(groups[0]),) + array.shape), groups)


def on_device(features, cotangent, w_qkv, w_out, cos_scale):
    feat = features.reshape(OWN, MODEL)
    cot = cotangent.reshape(OWN, MODEL)
    smem = pl.BlockSpec(memory_space=pltpu.SMEM)

    edge = jax.ShapeDtypeStruct((SENT, MODEL), BF16)
    tile = jnp.concatenate([feat, cot])
    own_edge, mate_message = pl.pallas_call(
        edge_kernel,
        out_shape=(edge, jax.ShapeDtypeStruct((SENT + 144, MODEL), BF16)),
        in_specs=vmem(1),
        out_specs=vmem(2),
        compiler_params=pltpu.CompilerParams(vmem_limit_bytes=2 * 1024 * 1024),
        name="edges",
    )(tile)
    mate = lax.ppermute(mate_message, EVERY, CHIP_MATE)
    other_edge = mate[:SENT]
    far = lax.ppermute(jnp.concatenate([own_edge, other_edge]), EVERY, FAR_MATE)
    key_spots = np.zeros((2, 16, KEYS), np.float32)
    key_spots[:, :2] = TABLES
    key_spots = jnp.asarray(key_spots)
    scales = jnp.broadcast_to(cos_scale[None, :, None], (4, 2, MODEL)).reshape(8, MODEL)
    tile_copy, weights, bias, near_kv, near_q, near_d = pl.pallas_call(
        prepare_kernel,
        out_shape=(
            jax.ShapeDtypeStruct((2 * OWN, MODEL), BF16),
            jax.ShapeDtypeStruct((4 * MODEL, MODEL), BF16),
            jax.ShapeDtypeStruct((QUERIES, KEYS), F32),
            jax.ShapeDtypeStruct((224, 2 * MODEL), BF16),
            jax.ShapeDtypeStruct((176, MODEL), BF16),
            jax.ShapeDtypeStruct((176, MODEL), BF16),
        ),
        in_specs=vmem(5),
        out_specs=vmem(6),
        compiler_params=pltpu.CompilerParams(vmem_limit_bytes=4 * 1024 * 1024),
        cost_estimate=pl.CostEstimate(
            flops=1000000, bytes_accessed=1 << 20, transcendentals=0
        ),
        name="prepare",
    )(tile, mate, w_qkv, w_out, key_spots)
    next_chip = lax.ppermute(tile_copy, EVERY, NEXT_CHIP)

    far_mate = lax.ppermute(far, EVERY, CHIP_MATE)
    far_next = lax.ppermute(far, EVERY, NEXT_CHIP)
    far_skip = lax.ppermute(far, EVERY, SKIP_CHIP)
    grad_feat, grad_w, scale_tile = pl.pallas_call(
        attention_kernel,
        out_shape=(
            jax.ShapeDtypeStruct((OWN, MODEL), BF16),
            jax.ShapeDtypeStruct((4 * MODEL, MODEL), BF16),
            jax.ShapeDtypeStruct((8, MODEL), BF16),
        ),
        in_specs=vmem(12),
        out_specs=vmem(3),
        scratch_shapes=[
            pltpu.VMEM((KEYS, MODEL), BF16),
            pltpu.VMEM((QUERIES, MODEL), BF16),
            pltpu.VMEM((KEYS, MODEL), BF16),
            pltpu.VMEM((KEYS, MODEL), BF16),
            pltpu.VMEM((QUERIES, MODEL), BF16),
            pltpu.VMEM((QUERIES, MODEL), BF16),
            pltpu.VMEM((2, QUERIES, KEYS), F32),
            pltpu.VMEM((2, QUERIES, KEYS), F32),
            pltpu.VMEM((2, OWN, NEAR), BF16),
            pltpu.VMEM((2, QUERIES, OWN), BF16),
            pltpu.VMEM((2, OWN, NEAR), BF16),
            pltpu.VMEM((2, QUERIES, OWN), BF16),
        ],
        compiler_params=pltpu.CompilerParams(vmem_limit_bytes=16 * 1024 * 1024),
        name="window_attention",
    )(
        scales,
        tile,
        weights,
        near_kv,
        near_q,
        near_d,
        next_chip,
        far,
        far_skip,
        far_next,
        far_mate,
        bias,
    )

    scale_rows = jnp.broadcast_to(scale_tile[None, None, :2], (SHARES, 1, 2, MODEL))
    shares = jnp.concatenate([grad_w.reshape(SHARES, 8, 2, MODEL), scale_rows], axis=1)
    lane = lax.broadcasted_iota(jnp.int32, (2, MODEL), 1)
    shares, lane = lax.optimization_barrier((shares, lane))
    share = jnp.sum(exchange(shares, PLANES).astype(F32), axis=0)
    term = jnp.sum(jnp.where(lane < 3, share[8], 0.0), axis=1, keepdims=True)
    top = lax.reduce_precision(term, 8, 7)
    middle = lax.reduce_precision(term - top, 8, 7)
    parts = jnp.where(lane == 0, top, jnp.where(lane == 1, middle, term - top - middle))
    parts = jnp.where(lane < 3, parts, 0.0)
    share = jnp.concatenate([share[:8], parts[None]], axis=0).astype(BF16)
    share = jnp.sum(to_all(share, LINES).astype(F32), axis=0)
    share, terms = lax.optimization_barrier((share[:8].astype(BF16).reshape(16, MODEL), share[8]))
    whole = to_all(share, PLANES).reshape(4 * MODEL, MODEL)
    grad_feat, grad_w_qkv, grad_w_out, grad_scale = pl.pallas_call(
        result_kernel,
        out_shape=(
            jax.ShapeDtypeStruct((OWN, MODEL), BF16),
            jax.ShapeDtypeStruct((MODEL, 3 * MODEL), F32),
            jax.ShapeDtypeStruct((MODEL, MODEL), F32),
            jax.ShapeDtypeStruct((2,), F32),
        ),
        in_specs=vmem(3),
        out_specs=vmem(3) + [smem],
        compiler_params=pltpu.CompilerParams(vmem_limit_bytes=2 * 1024 * 1024),
        name="results",
    )(whole, terms, grad_feat)
    return (grad_feat.reshape(ROWS, COLS, MODEL), grad_w_qkv, grad_w_out, grad_scale)


def solution(mesh):
    tokens = P("row", "col", None)
    return jax.shard_map(
        on_device,
        mesh=mesh,
        in_specs=(tokens, tokens, P(), P(), P()),
        out_specs=(tokens, P(), P(), P()),
        check_vma=False,
    )
```
